256 devices in a mesh: expert: 32 (over z, y), hidden: 8 (over x, core).
Axes of the slice: x: 4, y: 4, z: 8, core: 2. Of those that a mesh axis runs over, the one named last changes fastest.
Arguments:
- tokens: bfloat16 [1024, 7168], P('expert'), may hold values from -6 to 6
- grad_out: bfloat16 [1024, 7168], P('expert'), may hold values from -1.5 to 1.5
- routes: int32 [1024, 8], P('expert'), may hold values from 0 to 31, all different within a row; in each aligned block of 32 rows (0 to 31, 32 to 63, ...) at most 16 rows name the same one
- gating: bfloat16 [1024, 8], P('expert'), may hold values from 0.19921875 to 1
- w_gate: bfloat16 [32, 7168, 1024], P('expert', None, 'hidden'), may hold values from -0.0625 to 0.0625
- w_up: bfloat16 [32, 7168, 1024], P('expert', None, 'hidden'), may hold values from -0.0625 to 0.0625
- w_down: bfloat16 [32, 1024, 7168], P('expert', 'hidden'), may hold values from -0.1875 to 0.1875
Outputs:
- grad_tokens: bfloat16 [1024, 7168], P('expert', 'hidden')
- grad_gating: float32 [1024, 8], P('expert')
- grad_w_gate: bfloat16 [32, 7168, 1024], P('expert', None, 'hidden')
- grad_w_up: bfloat16 [32, 7168, 1024], P('expert', None, 'hidden')
- grad_w_down: bfloat16 [32, 1024, 7168], P('expert', 'hidden')
The draws below stay inside these ranges and needn't reach their ends.
Inputs may be any that keep to these rules, and one draw needn't show every extreme that they name: `routes`: each row names 8 different experts; in the rows of one token owner no expert is named by more than 16 rows, and in some owners' rows an expert is named by exactly 16 rows. Every expert is named somewhere.
All inputs are finite; a program needn't handle non-finite values.
Results may differ from the reference program's by a relative error of at most 0.019.
Values may be sent and summed in bfloat16 or wider, within the bound.
No kernel may reach another device: no remote copies, remote signals or barrier semaphores. Data moves between devices by JAX's collectives and lax.ppermute only.
A program may use at most 192 MiB of HBM per device.

```python
import math
import jax
import jax.numpy as jnp
import numpy as np
from jax import lax

D = 7168
H = 1024
TOPK = 8
TOK_DEV = 32
EXPERTS = 32
CAP = 16
TOKENS = 1024
N_EXPERT = 32
N_HIDDEN = 8


def block_scale(key, dims, cuts, smallest, largest):
    level = 1.0
    for axis_at, shards_of in cuts:
        steps = jax.random.uniform(jax.random.fold_in(jax.random.fold_in(key, 6), axis_at), (shards_of,), jnp.float32, smallest / len(cuts), largest / len(cuts))
        level = level * jnp.repeat(jnp.exp(steps), dims[axis_at] // shards_of).reshape((-1,) + (1,) * (len(dims) - 1 - axis_at))
    return level


def deal_out(rng, own, number, rows, amount, top, bound, slope):
    order = jax.random.permutation(rng, amount)
    crowded, usual = shares(amount, rows * top, bound, slope, True), shares(amount, rows * top, bound, slope, False)
    places = jnp.arange(amount)

    def named(lengths, turn):
        used = int((lengths > 0).sum())
        fixed = max(1, used // 4)
        moved = fixed + (places - fixed + turn * (used - fixed)) % max(1, amount - fixed)
        return jnp.zeros((amount,), jnp.int32).at[order[jnp.where(places < fixed, places, moved)]].set(jnp.asarray(lengths, jnp.int32))

    lengths = jnp.where(number % 4 == 0, named(crowded, number // 4), named(usual, number - number // 4 - 1))
    mixed = jax.random.permutation(jax.random.fold_in(own, 3), amount)
    giver, receiver = mixed[0:amount // 2 * 2:2], mixed[1:amount // 2 * 2:2]
    margin = jnp.minimum(lengths[giver] - 1, bound - lengths[receiver]) // 2
    margin = jnp.where((giver == order[0]) | (receiver == order[0]) | (lengths[receiver] == 0), 0, jnp.maximum(margin, 0))
    moved = jax.random.randint(jax.random.fold_in(own, 4), (amount // 2,), 0, 1 << 20) % (margin + 1)
    lengths = lengths.at[giver].add(-moved).at[receiver].add(moved)
    labels = jnp.searchsorted(jnp.cumsum(lengths), jnp.arange(rows * top), side="right").astype(jnp.int32)
    grid = labels.reshape(top, rows).T
    grid = grid[jax.random.permutation(jax.random.fold_in(own, 1), rows)]
    turn = jax.random.randint(jax.random.fold_in(own, 2), (rows, 1), 0, top)
    return jnp.take_along_axis(grid, (jnp.arange(top)[None, :] + turn) % top, axis=1)


def shares(number_of, total, bound, slope, full):
    weights = [(1 << 20) // math.isqrt(grade ** slope) + 1 for grade in range(1, number_of + 1)]
    largest = bound if full else min(bound, max(-(-total // number_of), total * weights[0] // sum(weights)))
    least = 1 if total - largest >= number_of - 1 else 0
    holding, spare = [largest] + [least] * (number_of - 1), total - largest - least * (number_of - 1)
    while spare > 0:
        free = [i for i in range(1, number_of) if holding[i] < largest] or [i for i in range(1, number_of) if holding[i] < bound]
        whole, budget = sum([weights[i] for i in free]), spare
        for i in free:
            extra = min(bound - holding[i], max(1, budget * weights[i] // whole), spare)
            holding[i] = holding[i] + extra
            spare = spare - extra
    return np.array(holding)


def noise(own_key, extent, width, bound, cuts=(), held_as=jnp.bfloat16):
    values = width * jax.random.normal(own_key, extent, jnp.float32)
    if cuts:
        values = values * block_scale(own_key, extent, cuts, -0.22, 0.18)
    return jnp.clip(values, -bound, bound).astype(held_as)


def setup_inputs(seed: int = 0) -> dict:
    key_of = jax.random.split(jax.random.key(seed), 8)
    tokens = noise(key_of[0], (TOKENS, D), 1.0, 6.0, ((0, 32),))
    grad_out = noise(key_of[1], (TOKENS, D), 0.25, 1.5, ((0, 32),))
    routes_keys = jax.random.split(jax.random.fold_in(key_of[2], 1), TOKENS // TOK_DEV)
    routes_turns = jax.random.permutation(jax.random.fold_in(key_of[2], 3), TOKENS // TOK_DEV)
    routes = jax.vmap(lambda own, number: deal_out(jax.random.fold_in(key_of[2], 2), own, number, TOK_DEV, EXPERTS, TOPK, CAP, 2))(routes_keys, routes_turns).reshape((TOKENS, TOPK))
    gating = jnp.clip(0.19921875 + 0.80078125 * jax.random.uniform(key_of[3], (TOKENS, TOPK), jnp.float32) ** block_scale(key_of[3], (TOKENS, TOPK), ((0, 32),), -0.2, 0.2), 0.19921875, 1.0).astype(jnp.bfloat16)
    w_gate = noise(key_of[4], (EXPERTS, D, H), D ** -0.5, 0.0625, ((0, 32), (2, 8)))
    w_up = noise(key_of[5], (EXPERTS, D, H), D ** -0.5, 0.0625, ((0, 32), (2, 8)))
    w_down = noise(key_of[6], (EXPERTS, H, D), H ** -0.5, 0.1875, ((0, 32), (1, 8)))
    return dict(tokens=tokens, grad_out=grad_out, routes=routes, gating=gating, w_gate=w_gate, w_up=w_up, w_down=w_down)


def silu_parts(pre):
    sig = jax.nn.sigmoid(pre)
    return pre * sig, sig * (1.0 + pre * (1.0 - sig))


def reference(tokens, grad_out, routes, gating, w_gate, w_up, w_down):
    blocks = routes.reshape(N_EXPERT, TOK_DEV * TOPK)
    onehot = (blocks[:, :, None] == jnp.arange(EXPERTS, dtype=jnp.int32)[None, None, :]).astype(jnp.int32)
    before = jnp.cumsum(onehot, axis=1) - onehot
    slots = jnp.sum(before * onehot, axis=2).astype(jnp.int32)
    source = jnp.broadcast_to(jnp.arange(N_EXPERT, dtype=jnp.int32)[:, None], blocks.shape)
    place = ((blocks * N_EXPERT + source) * CAP + slots).reshape(-1).astype(jnp.int32)
    token_ids = jnp.repeat(jnp.arange(TOKENS, dtype=jnp.int32), TOPK)
    table = jnp.full((EXPERTS * N_EXPERT * CAP,), TOKENS, jnp.int32).at[place].set(token_ids)
    gate_table = jnp.zeros((EXPERTS * N_EXPERT * CAP,), jnp.float32).at[place].set(gating.reshape(-1).astype(jnp.float32))
    table = table.reshape(EXPERTS, N_EXPERT * CAP)
    gate_table = gate_table.reshape(EXPERTS, N_EXPERT * CAP)
    padded_x = jnp.concatenate([tokens, jnp.zeros((1, D), tokens.dtype)], axis=0)
    padded_dy = jnp.concatenate([grad_out, jnp.zeros((1, D), grad_out.dtype)], axis=0)
    part_width = H // N_HIDDEN

    def one_expert(total, inputs):
        index, gate_col, wgate, wup, wdown = inputs
        rows_x = padded_x[index]
        rows_dy = padded_dy[index]
        pre_gate = jnp.dot(rows_x, wgate, preferred_element_type=jnp.float32)
        pre_up = jnp.dot(rows_x, wup, preferred_element_type=jnp.float32)
        back = lax.dot_general(rows_dy, wdown, (((1,), (1,)), ((), ())), preferred_element_type=jnp.float32)
        silu_val, silu_grad = silu_parts(pre_gate)
        act = silu_val * pre_up
        gate_grad = jnp.sum(act * back, axis=1)
        weight_col = gate_col[:, None]
        weighted = (weight_col * act).astype(jnp.bfloat16)
        grad_wd = lax.dot_general(weighted, rows_dy, (((0,), (0,)), ((), ())), preferred_element_type=jnp.float32).astype(jnp.bfloat16)
        dact = weight_col * back
        d_up = (dact * silu_val).astype(jnp.bfloat16)
        d_gate = (dact * pre_up * silu_grad).astype(jnp.bfloat16)
        grad_wg = lax.dot_general(rows_x, d_gate, (((0,), (0,)), ((), ())), preferred_element_type=jnp.float32).astype(jnp.bfloat16)
        grad_wu = lax.dot_general(rows_x, d_up, (((0,), (0,)), ((), ())), preferred_element_type=jnp.float32).astype(jnp.bfloat16)
        rows = index.shape[0]
        parts = jnp.einsum("chk,dhk->hcd", d_gate.reshape(rows, N_HIDDEN, part_width).astype(jnp.float32),
                           wgate.reshape(D, N_HIDDEN, part_width).astype(jnp.float32), precision=lax.Precision.HIGHEST)
        parts = parts + jnp.einsum("chk,dhk->hcd", d_up.reshape(rows, N_HIDDEN, part_width).astype(jnp.float32),
                                   wup.reshape(D, N_HIDDEN, part_width).astype(jnp.float32), precision=lax.Precision.HIGHEST)
        rounded = lax.optimization_barrier(parts.astype(jnp.bfloat16)).astype(jnp.float32)
        row_grad = jnp.sum(rounded, axis=0)
        total = total.at[index].add(row_grad)
        return total, (gate_grad, grad_wg, grad_wu, grad_wd)

    start = jnp.zeros((TOKENS + 1, D), jnp.float32)
    total, outputs = lax.scan(one_expert, start, (table, gate_table, w_gate, w_up, w_down))
    gate_grads, grad_w_gate, grad_w_up, grad_w_down = outputs
    grad_tokens = total[:TOKENS].astype(jnp.bfloat16)
    grad_gating = gate_grads.reshape(-1)[place].reshape(TOKENS, TOPK)
    return grad_tokens, grad_gating, grad_w_gate, grad_w_up, grad_w_down
```

```python
import functools

import jax
import jax.numpy as jnp
from jax import lax
from jax.experimental import pallas as pl
from jax.experimental.pallas import tpu as pltpu
from jax.sharding import PartitionSpec as P

CAP = 16
CHIPS = 4
BF = jnp.bfloat16
F32 = jnp.float32
VMEM_LIMIT = 40 * 1024 * 1024

NN = (((1,), (0,)), ((), ()))
NT = (((1,), (1,)), ((), ()))
TN = (((0,), (0,)), ((), ()))


def mm(a, b, dims):
    return lax.dot_general(a, b, dims, preferred_element_type=F32)


def call(body, out_shape, flops=0, moved=0, **kw):
    return pl.pallas_call(
        body,
        out_shape=out_shape,
        compiler_params=pltpu.CompilerParams(vmem_limit_bytes=VMEM_LIMIT),
        cost_estimate=pl.CostEstimate(flops=flops, bytes_accessed=moved, transcendentals=0),
        **kw,
    )


def shape(dims, dtype):
    return jax.ShapeDtypeStruct(dims, dtype)


VM = pl.BlockSpec(memory_space=pltpu.VMEM)
SM = pl.BlockSpec(memory_space=pltpu.SMEM)


def select_rows(routes, gates, rows, experts):
    count, topk = routes.shape
    lane = lax.broadcasted_iota(jnp.int32, (count, experts), 1)
    named = jnp.zeros((count, experts), F32)
    weight = jnp.zeros((count, experts), F32)
    for k in range(topk):
        hit = routes[:, k : k + 1] == lane
        named = jnp.where(hit, 1.0, named)
        weight = jnp.where(hit, gates[:, k : k + 1].astype(F32), weight)
    earlier = (
        lax.broadcasted_iota(jnp.int32, (count, count), 1) < lax.broadcasted_iota(jnp.int32, (count, count), 0)
    ).astype(F32)
    slot = mm(earlier.astype(BF), named.astype(BF), NN)
    slot = jnp.where(named > 0, slot, 2.0 * CAP)
    row = lax.broadcasted_iota(jnp.int32, (rows, experts), 0)
    owner = (row // CAP == lax.broadcasted_iota(jnp.int32, (rows, experts), 1)).astype(F32).astype(BF)
    slot_of = mm(owner, slot.astype(BF), NT)
    weight_of = mm(owner, weight.astype(BF), NT)
    place = (lax.broadcasted_iota(jnp.int32, (rows, count), 0) % CAP).astype(F32)
    pick = jnp.where(slot_of == place, 1.0, 0.0)
    return pick, pick * weight_of


def prepare_body(experts, at, routes, gates, x, dy, send_x, send_dy):
    rows = send_x.shape[0]
    pick, weighted = select_rows(routes[...], gates[...], rows, experts)
    send_x[...] = mm(pick.astype(BF), x[...], NN).astype(BF)
    send_dy[...] = mm(weighted.astype(BF), dy[...], NN).astype(BF)


def prepare(at, routes, gates, tokens, grad_out, experts):
    count, width = tokens.shape
    block = width // (2 * CHIPS)
    rows = experts * CAP
    whole = lambda i, at: (0, 0)
    mine = lambda i, at: (0, 2 * at[0] + at[1])
    return call(
        functools.partial(prepare_body, experts),
        (shape((rows, block), BF), shape((rows, block), BF)),
        flops=4 * rows * count * block,
        moved=8 * rows * block,
        grid_spec=pltpu.PrefetchScalarGridSpec(
            num_scalar_prefetch=1,
            grid=(1,),
            in_specs=[
                pl.BlockSpec(routes.shape, whole),
                pl.BlockSpec(gates.shape, whole),
                pl.BlockSpec((count, block), mine),
                pl.BlockSpec((count, block), mine),
            ],
            out_specs=[pl.BlockSpec((rows, block), whole), pl.BlockSpec((rows, block), whole)],
        ),
    )(at, routes, gates, tokens, grad_out)


def copy_body(at, *refs):
    half = len(refs) // 2
    for source, target in zip(refs[:half], refs[half:]):
        target[0] = source[...]


def halves(at, w_gate, w_up, w_down):
    depth, units = w_gate.shape
    block = depth // (2 * CHIPS)
    other = lambda r, at: 2 * ((at[0] + r) % CHIPS) + 1 - at[1]
    down = pl.BlockSpec((block, units), lambda r, at: (other(r, at), 0))
    wide = pl.BlockSpec((units, block), lambda r, at: (0, other(r, at)))
    out = pl.BlockSpec((1, block, units), lambda r, at: (r, 0, 0))
    out_wide = pl.BlockSpec((1, units, block), lambda r, at: (r, 0, 0))
    return call(
        copy_body,
        (
            shape((CHIPS, block, units), BF),
            shape((CHIPS, block, units), BF),
            shape((CHIPS, units, block), BF),
        ),
        moved=12 * CHIPS * block * units,
        grid_spec=pltpu.PrefetchScalarGridSpec(
            num_scalar_prefetch=1,
            grid=(CHIPS,),
            in_specs=[down, down, wide],
            out_specs=[out, out, out_wide],
        ),
    )(at, w_gate, w_up, w_down)


def block_at(at, r):
    return 2 * lax.rem(at[0] + r, CHIPS) + at[1]


def tall(ref, at, r, block):
    return ref[pl.ds(pl.multiple_of(block_at(at, r) * block, 128), block), :]


def wide(ref, at, r, block):
    return ref[:, pl.ds(pl.multiple_of(block_at(at, r) * block, 128), block)]


def pre_weights(at, gate, up, gate_other, up_other, r, block):
    return jnp.concatenate(
        [tall(gate, at, r, block), gate_other[r], tall(up, at, r, block), up_other[r]], axis=1
    )


def blocks_of(own, right, left, opp_a, opp_b, lo, hi, half):
    far = opp_a[...] if lo < half else opp_b[...]
    return (own[lo:hi, :], right[lo:hi, :], far, left[lo:hi, :])


def pre_body(at, own, right, left, opp_a, opp_b, gate, up, gate_other, up_other, keep, send):
    rows, block = own.shape
    half = rows // 2
    units = gate.shape[1]
    for r in range(CHIPS):
        weights = pre_weights(at, gate, up, gate_other, up_other, r, block)
        for lo in (0, half):
            part = mm(blocks_of(own, right, left, opp_a, opp_b, lo, lo + half, half)[r], weights, NN)
            if r == 0:
                keep[lo : lo + half, :] = part
            else:
                keep[lo : lo + half, :] += part
    for i, j in ((0, 1), (1, 0), (2, 3), (3, 2)):
        send[:, i * units : (i + 1) * units] = keep[:, j * units : (j + 1) * units]


def back_body(at, own, right, left, opp_a, opp_b, down, down_other, keep, send):
    rows, block = own.shape
    half = rows // 2
    units = down.shape[0]
    for r in range(CHIPS):
        weights = jnp.concatenate([wide(down, at, r, block), down_other[r]], axis=0)
        for lo in (0, half):
            part = mm(blocks_of(own, right, left, opp_a, opp_b, lo, lo + half, half)[r], weights, NT)
            if r == 0:
                keep[lo : lo + half, :] = part
            else:
                keep[lo : lo + half, :] += part
    send[:, :units] = keep[:, units:]
    send[:, units:] = keep[:, :units]


def middle_body(
    at, pre, pre_recv, back, back_recv, gate, up, gate_other, up_other, d, weighted, sums, opp_a, opp_b
):
    rows = pre.shape[0]
    both = pre.shape[1] // 2
    half = rows // 2
    block = opp_a.shape[1]
    weights = pre_weights(at, gate, up, gate_other, up_other, 2, block)
    ones = jnp.ones((8, both), F32)
    for lo, out in ((0, opp_a), (half, opp_b)):
        span = slice(lo, lo + half)
        pre_all = pre[span, :] + pre_recv[span, :]
        back_all = back[span, :] + back_recv[span, :]
        pre_gate = pre_all[:, :both]
        pre_up = pre_all[:, both:]
        sig = jax.nn.sigmoid(pre_gate)
        silu = pre_gate * sig
        act = silu * pre_up
        sums[:, span] = lax.dot_general(
            ones, act * back_all, NT, preferred_element_type=F32, precision=lax.Precision.HIGHEST
        )
        weighted[span, :] = act.astype(BF)
        d_gate = (back_all * pre_up * (sig * (1.0 + pre_gate * (1.0 - sig)))).astype(BF)
        d_up = (back_all * silu).astype(BF)
        grads = jnp.concatenate([d_gate, d_up], axis=1)
        d[span, :] = grads
        out[...] = mm(grads, weights, NT).astype(BF)


def rows_body(at, d, gate, up, gate_other, up_other, to_right, to_left, right_later, left_later, own):
    rows = d.shape[0]
    half = rows // 2
    block = own.shape[1]
    weights = pre_weights(at, gate, up, gate_other, up_other, 1, block)
    to_right[...] = mm(d[half:, :], weights, NT).astype(BF)
    right_later[...] = mm(d[:half, :], weights, NT)
    weights = pre_weights(at, gate, up, gate_other, up_other, 3, block)
    to_left[...] = mm(d[:half, :], weights, NT).astype(BF)
    left_later[...] = mm(d[half:, :], weights, NT)
    weights = pre_weights(at, gate, up, gate_other, up_other, 0, block)
    own[:half, :] = mm(d[:half, :], weights, NT)
    own[half:, :] = mm(d[half:, :], weights, NT)


def grads_body(own, right, left, opp_a, opp_b, d, gate_own, gate_other, up_own, up_other):
    half = own.shape[0] // 2
    units = d.shape[1] // 4
    for r in range(CHIPS):
        total = None
        for lo in (0, half):
            rows = blocks_of(own, right, left, opp_a, opp_b, lo, lo + half, half)[r]
            part = mm(rows, d[lo : lo + half, :], TN)
            total = part if total is None else total + part
        for i, out in enumerate((gate_own, gate_other, up_own, up_other)):
            out[r] = total[:, i * units : (i + 1) * units].astype(BF)


def down_body(own, right, left, opp_a, opp_b, weighted, down_own, down_other):
    half = own.shape[0] // 2
    units = weighted.shape[1] // 2
    for r in range(CHIPS):
        total = None
        for lo in (0, half):
            rows = blocks_of(own, right, left, opp_a, opp_b, lo, lo + half, half)[r]
            part = mm(weighted[lo : lo + half, :], rows, TN)
            total = part if total is None else total + part
        down_own[r] = total[:units, :].astype(BF)
        down_other[r] = total[units:, :].astype(BF)


def place_body(at, *refs):
    pairs = len(refs) // 3
    mine = lax.rem(pl.program_id(0), 2) == at[1]
    for own, other, target in zip(refs[:pairs], refs[pairs : 2 * pairs], refs[2 * pairs :]):

        @pl.when(mine)
        def _():
            target[...] = own[0]

        @pl.when(jnp.logical_not(mine))
        def _():
            target[...] = other[0]


def place(at, gate_own, up_own, down_own, gate_other, up_other, down_other):
    _, block, units = gate_own.shape
    depth = 2 * CHIPS * block
    where = lambda b, at: ((b // 2 + CHIPS - at[0]) % CHIPS, 0, 0)
    source = pl.BlockSpec((1, block, units), where)
    source_wide = pl.BlockSpec((1, units, block), where)
    return call(
        place_body,
        (shape((depth, units), BF), shape((depth, units), BF), shape((units, depth), BF)),
        moved=18 * depth * units,
        grid_spec=pltpu.PrefetchScalarGridSpec(
            num_scalar_prefetch=1,
            grid=(2 * CHIPS,),
            in_specs=[source, source, source_wide] * 2,
            out_specs=[
                pl.BlockSpec((block, units), lambda b, at: (b, 0)),
                pl.BlockSpec((block, units), lambda b, at: (b, 0)),
                pl.BlockSpec((units, block), lambda b, at: (0, b)),
            ],
        ),
    )(at, gate_own, up_own, down_own, gate_other, up_other, down_other)


def finish_body(experts, routes, gates, back, grad):
    pick, _ = select_rows(routes[...], gates[...], back.shape[0], experts)
    grad[...] = mm(pick.astype(BF), back[...], TN).astype(BF)


def gating_body(experts, routes, gates, sums, grad):
    count, topk = routes.shape
    rows = experts * CAP
    pick, _ = select_rows(routes[...], gates[...], rows, experts)
    row = lax.broadcasted_iota(jnp.int32, (rows, experts), 0) // CAP
    owner = (row == lax.broadcasted_iota(jnp.int32, (rows, experts), 1)).astype(F32)
    cap_of = (
        lax.broadcasted_iota(jnp.int32, (rows, CAP), 0) % CAP == lax.broadcasted_iota(jnp.int32, (rows, CAP), 1)
    ).astype(F32)
    spread = lax.dot_general(owner, sums[...], NN, preferred_element_type=F32, precision=lax.Precision.HIGHEST)
    value = jnp.sum(spread * cap_of, axis=1, keepdims=True)
    table = lax.dot_general(
        pick * value, owner, TN, preferred_element_type=F32, precision=lax.Precision.HIGHEST
    )
    lane = lax.broadcasted_iota(jnp.int32, (count, experts), 1)
    for k in range(topk):
        hit = routes[:, k : k + 1] == lane
        picked = jnp.sum(jnp.where(hit, table, 0.0), axis=1, keepdims=True)
        grad[:, k : k + 1] = picked / gates[:, k : k + 1].astype(F32)


def to(value, shift):
    size = 2 * CHIPS
    return lax.ppermute(value, "hidden", [(i, (i + 2 * shift) % size) for i in range(size)])


def swap(value):
    return lax.ppermute(value, "hidden", [(i, i ^ 1) for i in range(2 * CHIPS)])


def ring_gather(own):
    half = own.shape[0] // 2
    left = to(own, 1)
    right = to(own, -1)
    opp_a = to(left[:half], 1)
    opp_b = to(right[half:], -1)
    return own, right, left, opp_a, opp_b


def local(tokens, grad_out, routes, gating, w_gate, w_up, w_down):
    experts = lax.axis_size("expert")
    hidden = lax.axis_index("hidden")
    at = jnp.stack([hidden // 2, hidden % 2]).astype(jnp.int32)
    rows = experts * CAP
    half = rows // 2
    count, width = tokens.shape
    topk = routes.shape[1]
    block = width // (2 * CHIPS)
    gate, up, down = w_gate[0], w_up[0], w_down[0]
    units = gate.shape[1]
    both = 2 * units

    def over_experts(value):
        split = value.reshape(experts, value.shape[0] // experts, value.shape[1])
        return lax.all_to_all(split, "expert", split_axis=0, concat_axis=0, tiled=True).reshape(value.shape)

    send_x, send_dy = prepare(at, routes, gating, tokens, grad_out, experts)
    x = ring_gather(over_experts(send_x))
    dy = ring_gather(over_experts(send_dy))
    gate_other, up_other, down_other = [swap(v) for v in halves(at, gate, up, down)]
    weights = (gate, up, gate_other, up_other)

    work = 4 * rows * block * CHIPS * both
    pre, pre_send = call(
        pre_body,
        (shape((rows, 2 * both), F32), shape((rows, 2 * both), F32)),
        flops=work,
        moved=8 * rows * block,
        in_specs=[SM] + [VM] * 9,
        out_specs=(VM, VM),
    )(at, *x, *weights)
    pre_recv = swap(pre_send)
    back, back_send = call(
        back_body,
        (shape((rows, both), F32), shape((rows, both), F32)),
        flops=work // 2,
        moved=8 * rows * block,
        in_specs=[SM] + [VM] * 7,
        out_specs=(VM, VM),
    )(at, *dy, down, down_other)
    back_recv = swap(back_send)

    d, weighted, sums, opp_a, opp_b = call(
        middle_body,
        (
            shape((rows, 2 * both), BF),
            shape((rows, both), BF),
            shape((8, rows), F32),
            shape((half, block), BF),
            shape((half, block), BF),
        ),
        flops=work // 4,
        moved=8 * rows * block,
        in_specs=[SM] + [VM] * 8,
        out_specs=(VM,) * 5,
    )(at, pre, pre_recv, back, back_recv, *weights)
    from_left = to(opp_a, 1)
    from_right = to(opp_b, -1)
    to_right, to_left, right_later, left_later, own = call(
        rows_body,
        (
            shape((half, block), BF),
            shape((half, block), BF),
            shape((half, block), F32),
            shape((half, block), F32),
            shape((rows, block), F32),
        ),
        flops=3 * work // 4,
        moved=12 * rows * block,
        in_specs=[SM] + [VM] * 5,
        out_specs=(VM,) * 5,
    )(at, d, *weights)
    left_b = to(to_right, 1)
    right_a = to(to_left, -1)
    left_a = to((right_later + from_left.astype(F32)).astype(BF), 1)
    right_b = to((left_later + from_right.astype(F32)).astype(BF), -1)
    total_a = own[:half] + left_a.astype(F32) + right_a.astype(F32)
    total_b = own[half:] + left_b.astype(F32) + right_b.astype(F32)
    returned = over_experts(jnp.concatenate([total_a, total_b]).astype(BF))

    grad_gate, gate_send, grad_up, up_send = call(
        grads_body,
        (shape((CHIPS, block, units), BF),) * 4,
        flops=work,
        moved=8 * rows * block,
        in_specs=[VM] * 6,
        out_specs=(VM,) * 4,
    )(*x, d)
    grad_down, down_send = call(
        down_body,
        (shape((CHIPS, units, block), BF),) * 2,
        flops=work // 2,
        moved=8 * rows * block,
        in_specs=[VM] * 6,
        out_specs=(VM,) * 2,
    )(*dy, weighted)
    grads = place(
        at, grad_gate, grad_up, grad_down, swap(gate_send), swap(up_send), swap(down_send)
    )

    slots = lax.all_to_all(
        sums[0].reshape(experts, 1, CAP), "expert", split_axis=0, concat_axis=0, tiled=True
    ).reshape(experts, CAP)
    slots = slots + to(slots, 1)
    slots = slots + to(slots, 2)
    grad_gating = call(
        functools.partial(gating_body, experts),
        shape((count, topk), F32),
        in_specs=[VM] * 3,
        out_specs=VM,
    )(routes, gating, slots)
    grad_tokens = call(
        functools.partial(finish_body, experts),
        shape((count, block), BF),
        in_specs=[VM] * 3,
        out_specs=VM,
    )(routes, gating, returned)
    return (grad_tokens, grad_gating, grads[0][None], grads[1][None], grads[2][None])


def solution(mesh):
    placed = (
        P("expert", None),
        P("expert", None),
        P("expert", None),
        P("expert", None),
        P("expert", None, "hidden"),
        P("expert", None, "hidden"),
        P("expert", "hidden", None),
    )
    return jax.shard_map(
        local,
        mesh=mesh,
        in_specs=placed,
        out_specs=(
            P("expert", "hidden"),
            P("expert", None),
            P("expert", None, "hidden"),
            P("expert", None, "hidden"),
            P("expert", "hidden", None),
        ),
        check_vma=False,
    )
```

```python
import functools

import jax
import jax.numpy as jnp
from jax import lax
from jax.experimental import pallas as pl
from jax.experimental.pallas import tpu as pltpu
from jax.sharding import PartitionSpec as P

CAP = 16
CHIPS = 4
BF = jnp.bfloat16
F32 = jnp.float32
VMEM_LIMIT = 16 * 1024 * 1024


NN = (((1,), (0,)), ((), ()))
NT = (((1,), (1,)), ((), ()))
TN = (((0,), (0,)), ((), ()))


def mm(a, b, dims):
    return lax.dot_general(a, b, dims, preferred_element_type=F32)


def call(body, out_shape, operands, after=(), token=False, scratch=(), places=None, outs=None):
    count = len(operands)
    out_shape = tuple(out_shape)
    results = len(out_shape)
    ins = places or [SM] + [VM] * (count - 1)
    outs = outs or (VM,) * results

    moved = sum(v.size * v.dtype.itemsize for v in tuple(operands[1:]) + out_shape)

    def run(*refs):
        given, made = refs[:count], refs[count + len(after) :]
        if token:
            made[results][...] = jnp.zeros((8, 128), F32)
            made = made[:results] + made[results + 1 :]
        body(*given, *made)

    return pl.pallas_call(
        run,
        out_shape=out_shape + ((shape((8, 128), F32),) if token else ()),
        in_specs=list(ins) + [ANY] * len(after),
        out_specs=tuple(outs) + ((VM,) if token else ()),
        scratch_shapes=list(scratch),
        compiler_params=pltpu.CompilerParams(vmem_limit_bytes=VMEM_LIMIT),
        cost_estimate=pl.CostEstimate(flops=0, bytes_accessed=moved, transcendentals=0),
    )(*operands, *after)


def shape(dims, dtype):
    return jax.ShapeDtypeStruct(dims, dtype)


VM = pl.BlockSpec(memory_space=pltpu.VMEM)
SM = pl.BlockSpec(memory_space=pltpu.SMEM)
ANY = pl.BlockSpec(memory_space=pl.ANY)
HBM = pl.BlockSpec(memory_space=pltpu.HBM)


CUTS = (7, 14)


def plan(block):
    pieces = ([], [])
    start = 0
    for message, cut in enumerate(CUTS):
        end = 2 * block * cut // 14
        for kind in (0, 1):
            lo, hi = max(start, kind * block), min(end, (kind + 1) * block)
            if lo < hi:
                pieces[kind].append((message, lo - start, lo - kind * block, hi - lo))
        start = end
    return pieces


def widths(block):
    ends = [0] + [2 * block * cut // 14 for cut in CUTS]
    return [hi - lo for lo, hi in zip(ends, ends[1:])]


def owner_of(rows, experts):
    row = lax.broadcasted_iota(jnp.int32, (rows, experts), 0) // CAP
    return (row == lax.broadcasted_iota(jnp.int32, (rows, experts), 1)).astype(F32)


def slot_is(rows, count):
    row = lax.broadcasted_iota(jnp.int32, (rows, count), 0) % CAP
    return row == lax.broadcasted_iota(jnp.int32, (rows, count), 1)


def select_rows(routes, gates, rows, experts):
    topk, count = routes.shape
    expert = lax.broadcasted_iota(jnp.int32, (experts, count), 0)
    named = jnp.zeros((experts, count), F32)
    weight = jnp.zeros((experts, count), F32)
    for k in range(topk):
        hit = routes[k : k + 1, :] == expert
        named = jnp.where(hit, 1.0, named)
        weight = jnp.where(hit, gates[k : k + 1, :].astype(F32), weight)
    earlier = (
        lax.broadcasted_iota(jnp.int32, (count, count), 0) < lax.broadcasted_iota(jnp.int32, (count, count), 1)
    ).astype(F32)
    slot = mm(named.astype(BF), earlier.astype(BF), NN)
    slot = jnp.where(named > 0, slot, 2.0 * CAP)
    owner = owner_of(rows, experts).astype(BF)
    slot_of = mm(owner, slot.astype(BF), NN)
    weight_of = mm(owner, weight.astype(BF), NN)
    place = (lax.broadcasted_iota(jnp.int32, (rows, count), 0) % CAP).astype(F32)
    pick = jnp.where(slot_of == place, 1.0, 0.0)
    return pick, pick * weight_of


def first_body(experts, at, routes, gates, x, out, pick_out, weigh_out):
    pick, weighted = select_rows(routes[...], gates[...], pick_out.shape[0], experts)
    pick = pick.astype(BF)
    pick_out[...] = pick
    weigh_out[...] = weighted.astype(BF)
    out[...] = mm(pick, x[:, : out.shape[1]], NN).astype(BF)


def rest_body(at, pick, weighted, x, dy, *outs):
    for chosen, source, pieces in zip((pick, weighted), (x, dy), plan(x.shape[1])):
        for message, column, feature, many in pieces:
            if message > 0:
                value = mm(chosen[...], source[:, feature : feature + many], NN)
                outs[message - 1][:, column : column + many] = value.astype(BF)


def halves_body(at, gate, up, down, out):
    units, block = down.shape
    out[0, 0] = gate[...]
    out[0, 1] = up[...]
    for j in range(0, block, units):
        out[0, 2, j : j + units, :] = down[:, j : j + units]


def halves(at, w_gate, w_up, w_down):
    depth, units = w_gate.shape
    block = depth // (2 * CHIPS)
    other = lambda r, at: 2 * ((at[0] + r) % CHIPS) + 1 - at[1]
    tall = pl.BlockSpec((block, units), lambda r, at: (other(r, at), 0))
    wide = pl.BlockSpec((units, block), lambda r, at: (0, other(r, at)))
    return pl.pallas_call(
        halves_body,
        out_shape=shape((CHIPS, 3, block, units), BF),
        compiler_params=pltpu.CompilerParams(vmem_limit_bytes=VMEM_LIMIT),
        cost_estimate=pl.CostEstimate(flops=0, bytes_accessed=12 * depth * units, transcendentals=0),
        grid_spec=pltpu.PrefetchScalarGridSpec(
            num_scalar_prefetch=1,
            grid=(CHIPS,),
            in_specs=[tall, tall, wide],
            out_specs=pl.BlockSpec((1, 3, block, units), lambda r, at: (r, 0, 0, 0)),
        ),
    )(at, w_gate, w_up, w_down)


def block_at(at, r):
    return 2 * lax.rem(at[0] + r, CHIPS) + at[1]


def pre_weights(at, gate, up, others, r, lo, hi):
    block = others.shape[2]
    mine = pl.ds(pl.multiple_of(block_at(at, r) * block + lo, 128), hi - lo)
    return jnp.concatenate([gate[mine, :], others[r, 0, lo:hi, :], up[mine, :], others[r, 1, lo:hi, :]], axis=1)


def down_weights(at, down, others, r, lo, hi):
    units = down.shape[0]
    block = others.shape[2]
    mine = pl.ds(pl.multiple_of(block_at(at, r) * block + lo, 128), hi - lo)
    other = [others[r, 2, j : j + units, :] for j in range(lo, hi, units)]
    return jnp.concatenate([down[:, mine], jnp.concatenate(other, axis=1)], axis=0)


def halves_of(parts, r, half, columns):
    if r == 2:
        return ((0, parts[3][:, columns]), (half, parts[4][:, columns]))
    ref = parts[{0: 0, 1: 1, 3: 2}[r]]
    return ((0, ref[:half, columns]), (half, ref[half:, columns]))


def send_swapped(keep, send, units):
    for i in range(keep.shape[1] // units):
        j = i ^ 1
        send[:, i * units : (i + 1) * units] = keep[:, j * units : (j + 1) * units]


def add_body(piece, which, first, last, pre, at, *refs):
    _, column, feature, many = piece
    columns = slice(column, column + many)
    weights, refs = (refs[:3], refs[3:]) if pre else (refs[:2], refs[2:])
    given = 3 * (which[0] == 0) + 2 * (2 in which)
    parts, refs = refs[:given], refs[given:]
    parts = [None] * (5 - given) + list(parts) if which[0] == 2 else parts
    before, refs = (None, refs) if first else (refs[0], refs[1:])
    keep = refs[0]
    half = keep.shape[0] // 2
    for r in which:
        cut = (feature, feature + many)
        block = pre_weights(at, *weights, r, *cut) if pre else down_weights(at, *weights, r, *cut)
        for lo, part in halves_of(parts, r, half, columns):
            value = mm(part, block, NN if pre else NT)
            if r == which[0]:
                keep[lo : lo + half, :] = value if first else before[lo : lo + half, :] + value
            else:
                keep[lo : lo + half, :] += value
    if last:
        send_swapped(keep, refs[1], weights[0].shape[1 if pre else 0])


def middle_body(at, pre, pre_recv, back, back_recv, gate, up, others, d, act_rows, sums, opp_a, opp_b):
    rows = pre.shape[0]
    both = pre.shape[1] // 2
    half = rows // 2
    experts = rows // CAP
    owner = owner_of(rows, experts)
    slot = slot_is(rows, CAP)
    weights = pre_weights(at, gate, up, others, 2, 0, opp_a.shape[1])
    total = None
    for lo, out in ((0, opp_a), (half, opp_b)):
        span = slice(lo, lo + half)
        pre_all = pre[span, :] + pre_recv[span, :]
        back_all = back[span, :] + back_recv[span, :]
        pre_gate = pre_all[:, :both]
        pre_up = pre_all[:, both:]
        sig = jax.nn.sigmoid(pre_gate)
        silu = pre_gate * sig
        act = silu * pre_up
        act_rows[span, :] = act.astype(BF)
        d_gate = (back_all * pre_up * (sig * (1.0 + pre_gate * (1.0 - sig)))).astype(BF)
        d_up = (back_all * silu).astype(BF)
        grads = jnp.concatenate([d_gate, d_up], axis=1)
        d[span, :] = grads
        out[...] = mm(grads, weights, NT).astype(BF)
        value = jnp.sum(act * back_all, axis=1, keepdims=True)
        part = lax.dot_general(
            owner[span, :],
            jnp.where(slot[span, :], value, 0.0),
            TN,
            preferred_element_type=F32,
            precision=lax.Precision.HIGHEST,
        )
        total = part if total is None else total + part
    sums[...] = total


def rows_body(at, d, gate, up, others, to_right, to_left, right_later, left_later, own):
    half = d.shape[0] // 2
    block = own.shape[1]
    weights = pre_weights(at, gate, up, others, 1, 0, block)
    to_right[...] = mm(d[half:, :], weights, NT).astype(BF)
    right_later[...] = mm(d[:half, :], weights, NT)
    weights = pre_weights(at, gate, up, others, 3, 0, block)
    to_left[...] = mm(d[:half, :], weights, NT).astype(BF)
    left_later[...] = mm(d[half:, :], weights, NT)
    weights = pre_weights(at, gate, up, others, 0, 0, block)
    own[:half, :] = mm(d[:half, :], weights, NT)
    own[half:, :] = mm(d[half:, :], weights, NT)


def later_body(at, right_later, left_later, from_left, from_right, to_right, to_left):
    to_right[...] = (right_later[...] + from_left[...].astype(F32)).astype(BF)
    to_left[...] = (left_later[...] + from_right[...].astype(F32)).astype(BF)


def total_body(at, own, left_a, left_b, right_a, right_b, out):
    half = own.shape[0] // 2
    for span, left, right in ((slice(0, half), left_a, right_a), (slice(half, 2 * half), left_b, right_b)):
        out[span, :] = (own[span, :] + left[...].astype(F32) + right[...].astype(F32)).astype(BF)


def grads_body(at, d, act_rows, *refs):
    keep, send = refs[-2:]
    messages = [refs[i : i + 5] for i in range(0, len(refs) - 2, 5)]
    block = keep.shape[2]
    units = keep.shape[3]
    half = d.shape[0] // 2
    tokens, cotangents = plan(block)
    for r in range(CHIPS):
        for message, column, feature, many in tokens:
            total = None
            for lo, part in halves_of(messages[message], r, half, slice(column, column + many)):
                value = mm(part, d[lo : lo + half, :], TN)
                total = value if total is None else total + value
            for i, (out, kind) in enumerate(((keep, 0), (send, 0), (keep, 1), (send, 1))):
                out[r, kind, feature : feature + many, :] = total[:, i * units : (i + 1) * units].astype(BF)
        for message, column, feature, many in cotangents:
            total = None
            for lo, part in halves_of(messages[message], r, half, slice(column, column + many)):
                value = mm(act_rows[lo : lo + half, :], part, TN)
                total = value if total is None else total + value
            total = total.astype(BF)
            for j in range(0, many, units):
                keep[r, 2, feature + j : feature + j + units, :] = total[:units, j : j + units]
                send[r, 2, feature + j : feature + j + units, :] = total[units:, j : j + units]


def place_body(at, keep, recv, gate, up, down, sems):
    block, units = keep.shape[2:]
    copies = []

    def add(source, target):
        copies.append(pltpu.make_async_copy(source, target, sems.at[len(copies)]))
        copies[-1].start()

    for r in range(CHIPS):
        for held, core in ((keep, at[1]), (recv, 1 - at[1])):
            start = pl.multiple_of((2 * lax.rem(at[0] + r, CHIPS) + core) * block, 128)
            add(held.at[r, 0], gate.at[pl.ds(start, block), :])
            add(held.at[r, 1], up.at[pl.ds(start, block), :])
            for j in range(0, block, units):
                add(held.at[r, 2, pl.ds(j, units)], down.at[:, pl.ds(pl.multiple_of(start + j, 128), units)])
    for copy in copies:
        copy.wait()


def finish_body(at, pick, back, grad):
    grad[...] = mm(pick[...], back[...], TN).astype(BF)


def gating_body(at, pick, routes, gates, sums, others, grad):
    topk, count = routes.shape
    rows = pick.shape[0]
    experts = rows // CAP
    owner = owner_of(rows, experts)
    spread = lax.dot_general(
        owner, sums[...] + others[...], NN, preferred_element_type=F32, precision=lax.Precision.HIGHEST
    )
    value = jnp.sum(jnp.where(slot_is(rows, CAP), spread, 0.0), axis=1, keepdims=True)
    table = lax.dot_general(
        owner, pick[...].astype(F32) * value, TN, preferred_element_type=F32, precision=lax.Precision.HIGHEST
    )
    expert = lax.broadcasted_iota(jnp.int32, (experts, count), 0)
    for k in range(topk):
        hit = routes[k : k + 1, :] == expert
        picked = jnp.sum(jnp.where(hit, table, 0.0), axis=0, keepdims=True)
        grad[k : k + 1, :] = picked / gates[k : k + 1, :].astype(F32)


def to(value, shift):
    size = 2 * CHIPS
    return lax.ppermute(value, "hidden", [(i, (i + 2 * shift) % size) for i in range(size)])


def swap(value):
    return lax.ppermute(value, "hidden", [(i, i ^ 1) for i in range(2 * CHIPS)])


def split_body(at, left, right, out_a, out_b):
    half = left.shape[0] // 2
    out_a[...] = left[:half, :]
    out_b[...] = right[half:, :]


def ring_gather(at, own, after):
    half = own.shape[0] // 2
    left = to(own, 1)
    right = to(own, -1)
    pass_a, pass_b, token = call(
        split_body,
        (shape((half, own.shape[1]), BF),) * 2,
        (at, left, right),
        after=after,
        token=True,
    )
    return (own, right, left, to(pass_a, 1), to(pass_b, -1)), (token,)


def behind(value, token):
    return pl.pallas_call(
        lambda *refs: None,
        out_shape=shape(value.shape, value.dtype),
        in_specs=[ANY, ANY],
        out_specs=ANY,
        input_output_aliases={0: 0},
        compiler_params=pltpu.CompilerParams(vmem_limit_bytes=VMEM_LIMIT // 4),
    )(value, token)


def local(tokens, grad_out, routes, gating, w_gate, w_up, w_down):
    experts = lax.axis_size("expert")
    hidden = lax.axis_index("hidden")
    at = jnp.stack([lax.shift_right_logical(hidden, 1), lax.bitwise_and(hidden, 1)]).astype(jnp.int32)
    rows = experts * CAP
    half = rows // 2
    count, width = tokens.shape
    topk = routes.shape[1]
    block = width // (2 * CHIPS)
    gate, up, down = w_gate[0], w_up[0], w_down[0]
    units = gate.shape[1]
    both = 2 * units
    routes, gates = routes.T, gating.T
    of_tokens, of_cotangents = plan(block)

    def over_experts(value):
        split = value.reshape(experts, value.shape[0] // experts, value.shape[1])
        return lax.all_to_all(split, "expert", split_axis=0, concat_axis=0, tiled=True).reshape(value.shape)

    def my_block(value):
        return lax.dynamic_slice(value, (0, hidden * block), (count, block))

    my_tokens = my_block(tokens)
    message, pick, weighted = call(
        functools.partial(first_body, experts),
        (shape((rows, widths(block)[0]), BF),) + (shape((rows, count), BF),) * 2,
        (at, routes, gates, my_tokens),
    )
    arrived = [over_experts(message)]
    messages = call(
        rest_body,
        tuple(shape((rows, many), BF) for many in widths(block)[1:]),
        (at, pick, weighted, my_tokens, my_block(grad_out)),
    )
    arrived += [over_experts(message) for message in messages]
    gathered = []
    token = ()
    for value in arrived:
        parts, token = ring_gather(at, value, token)
        gathered.append(parts)
    others = swap(halves(at, gate, up, down))
    weights = (gate, up, others)

    pre = ()
    for i, piece in enumerate(of_tokens):
        pre = call(
            functools.partial(add_body, piece, (0, 1, 3, 2), i == 0, i == len(of_tokens) - 1, True),
            (shape((rows, 2 * both), F32),) * (1 + (i == len(of_tokens) - 1)),
            (at, *weights, *gathered[piece[0]], *pre),
        )
    pre, pre_send = pre
    pre_recv = swap(pre_send)
    narrow = (shape((rows, both), F32),)
    back = ()
    turns = [(piece, (0, 1, 3, 2)) for piece in of_cotangents[:-1]]
    for piece, which in turns + [(of_cotangents[-1], (0, 1, 3)), (of_cotangents[-1], (2,))]:
        last = which == (2,)
        parts = gathered[piece[0]]
        parts = parts[3:] if last else parts[: 5 if 2 in which else 3]
        back = call(
            functools.partial(add_body, piece, which, not back, last, False),
            narrow * (1 + last),
            (at, down, others, *parts, *back),
        )
    back, back_send = back
    back_recv = swap(back_send)

    part = (shape((half, block), BF),)
    later = (shape((half, block), F32),)
    d, act_rows, sums, opp_a, opp_b = call(
        middle_body,
        (shape((rows, 2 * both), BF), shape((rows, both), BF), shape((experts, CAP), F32)) + part * 2,
        (at, pre, pre_recv, back, back_recv, *weights),
    )
    from_left, from_right = to(opp_a, 1), to(opp_b, -1)
    to_right, to_left, right_later, left_later, own, *token = call(
        rows_body,
        part * 2 + later * 2 + (shape((rows, block), F32),),
        (at, d, *weights),
        token=True,
    )
    left_b, right_a = to(to_right, 1), to(to_left, -1)
    keep, send, *token = call(
        grads_body,
        (shape((CHIPS, 3, block, units), BF),) * 2,
        (at, d, act_rows, *[part for parts in gathered for part in parts]),
        after=token,
        token=True,
    )
    to_right, to_left = call(later_body, part * 2, (at, right_later, left_later, from_left, from_right), after=token)
    left_a, right_b = to(to_right, 1), to(to_left, -1)
    slots = over_experts(sums)
    total, *token = call(
        total_body,
        (shape((rows, block), BF),),
        (at, own, left_a, left_b, right_a, right_b),
        after=(slots,),
        token=True,
    )
    returned = over_experts(total)
    *grads, placed = call(
        place_body,
        (shape((2 * CHIPS * block, units), BF),) * 2 + (shape((units, 2 * CHIPS * block), BF),),
        (at, keep, swap(behind(send, token[0]))),
        token=True,
        scratch=[pltpu.SemaphoreType.DMA((2 * CHIPS * (2 + block // units),))],
        places=[SM] + [ANY] * 2,
        outs=(HBM,) * 3,
    )

    slots = slots + to(slots, 1)
    grad_gating, gated = call(
        gating_body,
        (shape((topk, count), F32),),
        (at, pick, routes, gates, slots, to(slots, 2)),
        token=True,
    )
    (grad_tokens,) = call(
        finish_body,
        (shape((count, block), BF),),
        (at, pick, returned),
        after=(placed, gated),
    )
    return (grad_tokens, grad_gating.T, grads[0][None], grads[1][None], grads[2][None])


def solution(mesh):
    placed = (
        P("expert", None),
        P("expert", None),
        P("expert", None),
        P("expert", None),
        P("expert", None, "hidden"),
        P("expert", None, "hidden"),
        P("expert", "hidden", None),
    )
    return jax.shard_map(
        local,
        mesh=mesh,
        in_specs=placed,
        out_specs=(
            P("expert", "hidden"),
            P("expert", None),
            P("expert", None, "hidden"),
            P("expert", None, "hidden"),
            P("expert", "hidden", None),
        ),
        check_vma=False,
    )
```

```python
import functools

import jax
import jax.numpy as jnp
from jax import lax
from jax.experimental import pallas as pl
from jax.experimental.pallas import tpu as pltpu
from jax.sharding import PartitionSpec as P

CAP = 16
CHIPS = 4
BF = jnp.bfloat16
F32 = jnp.float32
VMEM_LIMIT = 16 * 1024 * 1024


NN = (((1,), (0,)), ((), ()))
NT = (((1,), (1,)), ((), ()))
TN = (((0,), (0,)), ((), ()))


def mm(a, b, dims):
    return lax.dot_general(a, b, dims, preferred_element_type=F32)


def call(body, out_shape, operands, after=(), token=False, scratch=(), places=None, outs=None):
    count = len(operands)
    out_shape = tuple(out_shape)
    results = len(out_shape)
    ins = places or [SM] + [VM] * (count - 1)
    outs = outs or (VM,) * results

    moved = sum(v.size * v.dtype.itemsize for v in tuple(operands[1:]) + out_shape)

    def run(*refs):
        given, made = refs[:count], refs[count + len(after) :]
        if token:
            made[results][...] = jnp.zeros((8, 128), F32)
            made = made[:results] + made[results + 1 :]
        body(*given, *made)

    return pl.pallas_call(
        run,
        out_shape=out_shape + ((shape((8, 128), F32),) if token else ()),
        in_specs=list(ins) + [ANY] * len(after),
        out_specs=tuple(outs) + ((VM,) if token else ()),
        scratch_shapes=list(scratch),
        compiler_params=pltpu.CompilerParams(vmem_limit_bytes=VMEM_LIMIT),
        cost_estimate=pl.CostEstimate(flops=0, bytes_accessed=moved, transcendentals=0),
    )(*operands, *after)


def shape(dims, dtype):
    return jax.ShapeDtypeStruct(dims, dtype)


VM = pl.BlockSpec(memory_space=pltpu.VMEM)
SM = pl.BlockSpec(memory_space=pltpu.SMEM)
ANY = pl.BlockSpec(memory_space=pl.ANY)


CUTS = (7, 14)


def plan(block):
    pieces = ([], [])
    start = 0
    for message, cut in enumerate(CUTS):
        end = 2 * block * cut // 14
        for kind in (0, 1):
            lo, hi = max(start, kind * block), min(end, (kind + 1) * block)
            if lo < hi:
                pieces[kind].append((message, lo - start, lo - kind * block, hi - lo))
        start = end
    return pieces


def widths(block):
    ends = [0] + [2 * block * cut // 14 for cut in CUTS]
    return [hi - lo for lo, hi in zip(ends, ends[1:])]


def owner_of(rows, experts):
    row = lax.broadcasted_iota(jnp.int32, (rows, experts), 0) // CAP
    return (row == lax.broadcasted_iota(jnp.int32, (rows, experts), 1)).astype(F32)


def slot_is(rows, count):
    row = lax.broadcasted_iota(jnp.int32, (rows, count), 0) % CAP
    return row == lax.broadcasted_iota(jnp.int32, (rows, count), 1)


def select_rows(routes, gates, rows, experts):
    topk, count = routes.shape
    expert = lax.broadcasted_iota(jnp.int32, (experts, count), 0)
    named = jnp.zeros((experts, count), F32)
    weight = jnp.zeros((experts, count), F32)
    for k in range(topk):
        hit = routes[k : k + 1, :] == expert
        named = jnp.where(hit, 1.0, named)
        weight = jnp.where(hit, gates[k : k + 1, :].astype(F32), weight)
    earlier = (
        lax.broadcasted_iota(jnp.int32, (count, count), 0) < lax.broadcasted_iota(jnp.int32, (count, count), 1)
    ).astype(F32)
    slot = mm(named.astype(BF), earlier.astype(BF), NN)
    slot = jnp.where(named > 0, slot, 2.0 * CAP)
    owner = owner_of(rows, experts).astype(BF)
    slot_of = mm(owner, slot.astype(BF), NN)
    weight_of = mm(owner, weight.astype(BF), NN)
    place = (lax.broadcasted_iota(jnp.int32, (rows, count), 0) % CAP).astype(F32)
    pick = jnp.where(slot_of == place, 1.0, 0.0)
    return pick, pick * weight_of


def first_body(experts, at, routes, gates, x, out, pick_out, weigh_out):
    pick, weighted = select_rows(routes[...], gates[...], pick_out.shape[0], experts)
    pick = pick.astype(BF)
    pick_out[...] = pick
    weigh_out[...] = weighted.astype(BF)
    out[...] = mm(pick, x[:, : out.shape[1]], NN).astype(BF)


def rest_body(at, pick, weighted, x, dy, *outs):
    for chosen, source, pieces in zip((pick, weighted), (x, dy), plan(x.shape[1])):
        for message, column, feature, many in pieces:
            if message > 0:
                value = mm(chosen[...], source[:, feature : feature + many], NN)
                outs[message - 1][:, column : column + many] = value.astype(BF)


def halves_body(at, gate, up, down, out, token):
    token[...] = jnp.zeros((8, 128), F32)
    units, block = down.shape
    out[0, 0] = gate[...]
    out[0, 1] = up[...]
    for j in range(0, block, units):
        out[0, 2, j : j + units, :] = down[:, j : j + units]


def halves(at, w_gate, w_up, w_down):
    depth, units = w_gate.shape
    block = depth // (2 * CHIPS)
    other = lambda r, at: 2 * ((at[0] + r) % CHIPS) + 1 - at[1]
    tall = pl.BlockSpec((block, units), lambda r, at: (other(r, at), 0))
    wide = pl.BlockSpec((units, block), lambda r, at: (0, other(r, at)))
    return pl.pallas_call(
        halves_body,
        out_shape=(shape((CHIPS, 3, block, units), BF), shape((8, 128), F32)),
        compiler_params=pltpu.CompilerParams(vmem_limit_bytes=VMEM_LIMIT),
        cost_estimate=pl.CostEstimate(flops=0, bytes_accessed=12 * depth * units, transcendentals=0),
        grid_spec=pltpu.PrefetchScalarGridSpec(
            num_scalar_prefetch=1,
            grid=(CHIPS,),
            in_specs=[tall, tall, wide],
            out_specs=[
                pl.BlockSpec((1, 3, block, units), lambda r, at: (r, 0, 0, 0)),
                pl.BlockSpec((8, 128), lambda r, at: (0, 0)),
            ],
        ),
    )(at, w_gate, w_up, w_down)


def block_at(at, r):
    return 2 * lax.rem(at[0] + r, CHIPS) + at[1]


def pre_weights(at, gate, up, others, r, lo, hi):
    block = others.shape[2]
    mine = pl.ds(pl.multiple_of(block_at(at, r) * block + lo, 128), hi - lo)
    return jnp.concatenate([gate[mine, :], others[r, 0, lo:hi, :], up[mine, :], others[r, 1, lo:hi, :]], axis=1)


def down_weights(at, down, others, r, lo, hi):
    units = down.shape[0]
    block = others.shape[2]
    mine = pl.ds(pl.multiple_of(block_at(at, r) * block + lo, 128), hi - lo)
    other = [others[r, 2, j : j + units, :] for j in range(lo, hi, units)]
    return jnp.concatenate([down[:, mine], jnp.concatenate(other, axis=1)], axis=0)


def halves_of(parts, r, half, columns):
    if r == 2:
        return ((0, parts[3][:, columns]), (half, parts[4][:, columns]))
    ref = parts[{0: 0, 1: 1, 3: 2}[r]]
    return ((0, ref[:half, columns]), (half, ref[half:, columns]))


def swapped(value, units):
    pieces = [value[:, i : i + units] for i in range(0, value.shape[1], units)]
    return jnp.concatenate([pieces[i ^ 1] for i in range(len(pieces))], axis=1).astype(BF)


def add_body(piece, which, first, pre, at, *refs):
    _, column, feature, many = piece
    columns = slice(column, column + many)
    weights, refs = (refs[:3], refs[3:]) if pre else (refs[:2], refs[2:])
    given = 3 * (which[0] == 0) + 2 * (2 in which)
    parts, refs = refs[:given], refs[given:]
    parts = [None] * (5 - given) + list(parts) if which[0] == 2 else parts
    before, refs = (None, refs) if first else (refs[0], refs[1:])
    keep = refs[0]
    half = keep.shape[0] // 2
    for r in which:
        cut = (feature, feature + many)
        block = pre_weights(at, *weights, r, *cut) if pre else down_weights(at, *weights, r, *cut)
        for lo, part in halves_of(parts, r, half, columns):
            value = mm(part, block, NN if pre else NT)
            if r == which[0]:
                keep[lo : lo + half, :] = value if first else before[lo : lo + half, :] + value
            else:
                keep[lo : lo + half, :] += value


def early_body(x_piece, dy_piece, at, gate, up, others, down, *refs):
    x, dy, (pre, back) = refs[:5], refs[5:8], refs[8:]
    add_body(x_piece, (0, 1, 3, 2), True, True, at, gate, up, others, *x, pre)
    add_body(dy_piece, (0, 1, 3), True, False, at, down, others, *dy, back)


def late_body(dy_piece, at, down, others, opp_a, opp_b, before, pre, back, send):
    add_body(dy_piece, (2,), False, False, at, down, others, opp_a, opp_b, before, back)
    units = down.shape[0]
    send[:, : 4 * units] = swapped(pre[...], units)
    send[:, 4 * units :] = swapped(back[...], units)


def middle_body(at, pre, back, recv, gate, up, others, d, act_rows, sums, opp_a, opp_b):
    rows = pre.shape[0]
    both = pre.shape[1] // 2
    half = rows // 2
    experts = rows // CAP
    owner = owner_of(rows, experts)
    slot = slot_is(rows, CAP)
    weights = pre_weights(at, gate, up, others, 2, 0, opp_a.shape[1])
    total = None
    for lo, out in ((0, opp_a), (half, opp_b)):
        span = slice(lo, lo + half)
        pre_all = pre[span, :] + recv[span, : 2 * both].astype(F32)
        back_all = back[span, :] + recv[span, 2 * both :].astype(F32)
        pre_gate = pre_all[:, :both]
        pre_up = pre_all[:, both:]
        sig = jax.nn.sigmoid(pre_gate)
        silu = pre_gate * sig
        act = silu * pre_up
        act_rows[span, :] = act.astype(BF)
        d_gate = (back_all * pre_up * (sig * (1.0 + pre_gate * (1.0 - sig)))).astype(BF)
        d_up = (back_all * silu).astype(BF)
        grads = jnp.concatenate([d_gate, d_up], axis=1)
        d[span, :] = grads
        out[...] = mm(grads, weights, NT).astype(BF)
        value = jnp.sum(act * back_all, axis=1, keepdims=True)
        part = lax.dot_general(
            owner[span, :],
            jnp.where(slot[span, :], value, 0.0),
            TN,
            preferred_element_type=F32,
            precision=lax.Precision.HIGHEST,
        )
        total = part if total is None else total + part
    sums[...] = total


def rows_body(at, d, gate, up, others, to_right, to_left, right_later, left_later, own):
    half = d.shape[0] // 2
    block = own.shape[1]
    weights = pre_weights(at, gate, up, others, 1, 0, block)
    to_right[...] = mm(d[half:, :], weights, NT).astype(BF)
    right_later[...] = mm(d[:half, :], weights, NT)
    weights = pre_weights(at, gate, up, others, 3, 0, block)
    to_left[...] = mm(d[:half, :], weights, NT).astype(BF)
    left_later[...] = mm(d[half:, :], weights, NT)
    weights = pre_weights(at, gate, up, others, 0, 0, block)
    own[:half, :] = mm(d[:half, :], weights, NT)
    own[half:, :] = mm(d[half:, :], weights, NT)


def later_body(at, right_later, left_later, from_left, from_right, to_right, to_left):
    to_right[...] = (right_later[...] + from_left[...].astype(F32)).astype(BF)
    to_left[...] = (left_later[...] + from_right[...].astype(F32)).astype(BF)


def total_body(at, own, left_a, left_b, right_a, right_b, out):
    half = own.shape[0] // 2
    for span, left, right in ((slice(0, half), left_a, right_a), (slice(half, 2 * half), left_b, right_b)):
        out[span, :] = (own[span, :] + left[...].astype(F32) + right[...].astype(F32)).astype(BF)


def grads_body(at, d, act_rows, *refs):
    keep, send = refs[-2:]
    messages = [refs[i : i + 5] for i in range(0, len(refs) - 2, 5)]
    block = keep.shape[2]
    units = keep.shape[3]
    half = d.shape[0] // 2
    tokens, cotangents = plan(block)
    for r in range(CHIPS):
        for message, column, feature, many in tokens:
            total = None
            for lo, part in halves_of(messages[message], r, half, slice(column, column + many)):
                value = mm(part, d[lo : lo + half, :], TN)
                total = value if total is None else total + value
            for i, (out, kind) in enumerate(((keep, 0), (send, 0), (keep, 1), (send, 1))):
                out[r, kind, feature : feature + many, :] = total[:, i * units : (i + 1) * units].astype(BF)
        for message, column, feature, many in cotangents:
            total = None
            for lo, part in halves_of(messages[message], r, half, slice(column, column + many)):
                value = mm(act_rows[lo : lo + half, :], part, TN)
                total = value if total is None else total + value
            total = total.astype(BF)
            for j in range(0, many, units):
                keep[r, 2, feature + j : feature + j + units, :] = total[:units, j : j + units]
                send[r, 2, feature + j : feature + j + units, :] = total[units:, j : j + units]


def place_body(at, keep, recv, gate, up, down, token):
    token[...] = jnp.zeros((8, 128), F32)
    units = gate.shape[1]
    mine = lax.rem(pl.program_id(0), 2) == at[1]

    def put(held):
        gate[...] = held[0, 0]
        up[...] = held[0, 1]
        for j in range(0, gate.shape[0], units):
            down[:, j : j + units] = held[0, 2, j : j + units, :]

    @pl.when(mine)
    def _():
        put(keep)

    @pl.when(jnp.logical_not(mine))
    def _():
        put(recv)


def place(at, keep, recv):
    _, _, block, units = keep.shape
    depth = 2 * CHIPS * block
    source = pl.BlockSpec((1, 3, block, units), lambda b, at: ((b // 2 + CHIPS - at[0]) % CHIPS, 0, 0, 0))
    return pl.pallas_call(
        place_body,
        out_shape=(
            shape((depth, units), BF),
            shape((depth, units), BF),
            shape((units, depth), BF),
            shape((8, 128), F32),
        ),
        compiler_params=pltpu.CompilerParams(vmem_limit_bytes=VMEM_LIMIT),
        cost_estimate=pl.CostEstimate(flops=0, bytes_accessed=12 * depth * units, transcendentals=0),
        grid_spec=pltpu.PrefetchScalarGridSpec(
            num_scalar_prefetch=1,
            grid=(2 * CHIPS,),
            in_specs=[source, source],
            out_specs=[
                pl.BlockSpec((block, units), lambda b, at: (b, 0)),
                pl.BlockSpec((block, units), lambda b, at: (b, 0)),
                pl.BlockSpec((units, block), lambda b, at: (0, b)),
                pl.BlockSpec((8, 128), lambda b, at: (0, 0)),
            ],
        ),
    )(at, keep, recv)


def finish_body(at, pick, back, grad):
    grad[...] = mm(pick[...], back[...], TN).astype(BF)


def gating_body(at, pick, routes, gates, sums, left, far, right, grad):
    topk, count = routes.shape
    rows = pick.shape[0]
    experts = rows // CAP
    owner = owner_of(rows, experts)
    spread = lax.dot_general(
        owner, sums[...] + left[...] + far[...] + right[...], NN, preferred_element_type=F32, precision=lax.Precision.HIGHEST
    )
    value = jnp.sum(jnp.where(slot_is(rows, CAP), spread, 0.0), axis=1, keepdims=True)
    table = lax.dot_general(
        owner, pick[...].astype(F32) * value, TN, preferred_element_type=F32, precision=lax.Precision.HIGHEST
    )
    expert = lax.broadcasted_iota(jnp.int32, (experts, count), 0)
    for k in range(topk):
        hit = routes[k : k + 1, :] == expert
        picked = jnp.sum(jnp.where(hit, table, 0.0), axis=0, keepdims=True)
        grad[k : k + 1, :] = picked / gates[k : k + 1, :].astype(F32)


def to(value, shift):
    size = 2 * CHIPS
    return lax.ppermute(value, "hidden", [(i, (i + 2 * shift) % size) for i in range(size)])


def swap(value):
    return lax.ppermute(value, "hidden", [(i, i ^ 1) for i in range(2 * CHIPS)])


def split_body(at, left, right, out_a, out_b):
    half = left.shape[0] // 2
    out_a[...] = left[:half, :]
    out_b[...] = right[half:, :]


def ring_gather(at, own, after):
    half = own.shape[0] // 2
    left = to(own, 1)
    right = to(own, -1)
    pass_a, pass_b, token = call(
        split_body,
        (shape((half, own.shape[1]), BF),) * 2,
        (at, left, right),
        after=after,
        token=True,
    )
    return (own, right, left, to(pass_a, 1), to(pass_b, -1)), (token,)


def behind(value, token):
    return pl.pallas_call(
        lambda *refs: None,
        out_shape=shape(value.shape, value.dtype),
        in_specs=[ANY, ANY],
        out_specs=ANY,
        input_output_aliases={0: 0},
        compiler_params=pltpu.CompilerParams(vmem_limit_bytes=VMEM_LIMIT // 4),
    )(value, token)


def local(tokens, grad_out, routes, gating, w_gate, w_up, w_down):
    experts = lax.axis_size("expert")
    hidden = lax.axis_index("hidden")
    at = jnp.stack([lax.shift_right_logical(hidden, 1), lax.bitwise_and(hidden, 1)]).astype(jnp.int32)
    rows = experts * CAP
    half = rows // 2
    count, width = tokens.shape
    topk = routes.shape[1]
    block = width // (2 * CHIPS)
    gate, up, down = w_gate[0], w_up[0], w_down[0]
    units = gate.shape[1]
    both = 2 * units
    routes, gates = routes.T, gating.T
    of_tokens, of_cotangents = plan(block)

    def over_experts(value):
        split = value.reshape(experts, value.shape[0] // experts, value.shape[1])
        return lax.all_to_all(split, "expert", split_axis=0, concat_axis=0, tiled=True).reshape(value.shape)

    def my_block(value):
        return lax.dynamic_slice(value, (0, hidden * block), (count, block))

    my_tokens = my_block(tokens)
    message, pick, weighted = call(
        functools.partial(first_body, experts),
        (shape((rows, widths(block)[0]), BF),) + (shape((rows, count), BF),) * 2,
        (at, routes, gates, my_tokens),
    )
    arrived = [over_experts(message)]
    halved, token = halves(at, gate, up, down)
    messages = call(
        rest_body,
        tuple(shape((rows, many), BF) for many in widths(block)[1:]),
        (at, pick, weighted, my_tokens, my_block(grad_out)),
        after=(token,),
    )
    arrived += [over_experts(message) for message in messages]
    gathered = []
    token = ()
    for value in arrived:
        parts, token = ring_gather(at, value, token)
        gathered.append(parts)
    others = swap(halved)
    weights = (gate, up, others)

    (x_piece,), (dy_piece,) = of_tokens, of_cotangents
    x, dy = gathered
    narrow = shape((rows, both), F32)
    pre, back = call(
        functools.partial(early_body, x_piece, dy_piece),
        (shape((rows, 2 * both), F32), narrow),
        (at, gate, up, others, down, *x, *dy[:3]),
        after=token,
    )
    back, send = call(
        functools.partial(late_body, dy_piece),
        (narrow, shape((rows, 3 * both), BF)),
        (at, down, others, *dy[3:], back, pre),
    )
    recv = swap(send)

    part = (shape((half, block), BF),)
    later = (shape((half, block), F32),)
    d, act_rows, sums, opp_a, opp_b = call(
        middle_body,
        (shape((rows, 2 * both), BF), shape((rows, both), BF), shape((experts, CAP), F32)) + part * 2,
        (at, pre, back, recv, *weights),
    )
    from_left, from_right = to(opp_a, 1), to(opp_b, -1)
    to_right, to_left, right_later, left_later, own, *token = call(
        rows_body,
        part * 2 + later * 2 + (shape((rows, block), F32),),
        (at, d, *weights),
        token=True,
    )
    left_b, right_a = to(to_right, 1), to(to_left, -1)
    keep, send, *token = call(
        grads_body,
        (shape((CHIPS, 3, block, units), BF),) * 2,
        (at, d, act_rows, *[part for parts in gathered for part in parts]),
        after=token,
        token=True,
    )
    to_right, to_left = call(later_body, part * 2, (at, right_later, left_later, from_left, from_right), after=token)
    left_a, right_b = to(to_right, 1), to(to_left, -1)
    slots = over_experts(sums)
    total, *token = call(
        total_body,
        (shape((rows, block), BF),),
        (at, own, left_a, left_b, right_a, right_b),
        after=(slots,),
        token=True,
    )
    returned = over_experts(total)
    *grads, placed = place(at, keep, swap(behind(send, token[0])))
    grad_gating, gated = call(
        gating_body,
        (shape((topk, count), F32),),
        (at, pick, routes, gates, slots, *[to(slots, shift) for shift in (1, 2, 3)]),
        token=True,
    )
    (grad_tokens,) = call(
        finish_body,
        (shape((count, block), BF),),
        (at, pick, returned),
        after=(gated, placed),
    )
    return (grad_tokens, grad_gating.T, grads[0][None], grads[1][None], grads[2][None])


def solution(mesh):
    placed = (
        P("expert", None),
        P("expert", None),
        P("expert", None),
        P("expert", None),
        P("expert", None, "hidden"),
        P("expert", None, "hidden"),
        P("expert", "hidden", None),
    )
    return jax.shard_map(
        local,
        mesh=mesh,
        in_specs=placed,
        out_specs=(
            P("expert", "hidden"),
            P("expert", None),
            P("expert", None, "hidden"),
            P("expert", None, "hidden"),
            P("expert", "hidden", None),
        ),
        check_vma=False,
    )
```

```python
import functools

import jax
import jax.numpy as jnp
from jax import lax
from jax.experimental import pallas as pl
from jax.experimental.pallas import tpu as pltpu
from jax.sharding import PartitionSpec as P

CAP = 16
CHIPS = 4
BF = jnp.bfloat16
F32 = jnp.float32
VMEM_LIMIT = 16 * 1024 * 1024


NN = (((1,), (0,)), ((), ()))
NT = (((1,), (1,)), ((), ()))
TN = (((0,), (0,)), ((), ()))


def mm(a, b, dims):
    return lax.dot_general(a, b, dims, preferred_element_type=F32)


def call(body, out_shape, operands, after=(), token=False, scratch=(), places=None, outs=None):
    count = len(operands)
    out_shape = tuple(out_shape)
    results = len(out_shape)
    ins = places or [SM] + [VM] * (count - 1)
    outs = outs or (VM,) * results

    moved = sum(v.size * v.dtype.itemsize for v in tuple(operands[1:]) + out_shape)

    def run(*refs):
        given, made = refs[:count], refs[count + len(after) :]
        if token:
            made[results][...] = jnp.zeros((8, 128), F32)
            made = made[:results] + made[results + 1 :]
        body(*given, *made)

    return pl.pallas_call(
        run,
        out_shape=out_shape + ((shape((8, 128), F32),) if token else ()),
        in_specs=list(ins) + [ANY] * len(after),
        out_specs=tuple(outs) + ((VM,) if token else ()),
        scratch_shapes=list(scratch),
        compiler_params=pltpu.CompilerParams(vmem_limit_bytes=VMEM_LIMIT),
        cost_estimate=pl.CostEstimate(flops=0, bytes_accessed=moved, transcendentals=0),
    )(*operands, *after)


def shape(dims, dtype):
    return jax.ShapeDtypeStruct(dims, dtype)


VM = pl.BlockSpec(memory_space=pltpu.VMEM)
SM = pl.BlockSpec(memory_space=pltpu.SMEM)
ANY = pl.BlockSpec(memory_space=pl.ANY)


CUTS = (7, 14)


def plan(block):
    pieces = ([], [])
    start = 0
    for message, cut in enumerate(CUTS):
        end = 2 * block * cut // 14
        for kind in (0, 1):
            lo, hi = max(start, kind * block), min(end, (kind + 1) * block)
            if lo < hi:
                pieces[kind].append((message, lo - start, lo - kind * block, hi - lo))
        start = end
    return pieces


def widths(block):
    ends = [0] + [2 * block * cut // 14 for cut in CUTS]
    return [hi - lo for lo, hi in zip(ends, ends[1:])]


def owner_of(rows, experts):
    row = lax.broadcasted_iota(jnp.int32, (rows, experts), 0) // CAP
    return (row == lax.broadcasted_iota(jnp.int32, (rows, experts), 1)).astype(F32)


def slot_is(rows, count):
    row = lax.broadcasted_iota(jnp.int32, (rows, count), 0) % CAP
    return row == lax.broadcasted_iota(jnp.int32, (rows, count), 1)


def select_rows(routes, gates, rows, experts):
    topk, count = routes.shape
    expert = lax.broadcasted_iota(jnp.int32, (experts, count), 0)
    named = jnp.zeros((experts, count), F32)
    weight = jnp.zeros((experts, count), F32)
    for k in range(topk):
        hit = routes[k : k + 1, :] == expert
        named = jnp.where(hit, 1.0, named)
        weight = jnp.where(hit, gates[k : k + 1, :].astype(F32), weight)
    earlier = (
        lax.broadcasted_iota(jnp.int32, (count, count), 0) < lax.broadcasted_iota(jnp.int32, (count, count), 1)
    ).astype(F32)
    slot = mm(named.astype(BF), earlier.astype(BF), NN)
    slot = jnp.where(named > 0, slot, 2.0 * CAP)
    owner = owner_of(rows, experts).astype(BF)
    slot_of = mm(owner, slot.astype(BF), NN)
    weight_of = mm(owner, weight.astype(BF), NN)
    place = (lax.broadcasted_iota(jnp.int32, (rows, count), 0) % CAP).astype(F32)
    pick = jnp.where(slot_of == place, 1.0, 0.0)
    return pick, pick * weight_of


def first_body(experts, at, routes, gates, x, out, pick_out, weigh_out):
    pick, weighted = select_rows(routes[...], gates[...], pick_out.shape[0], experts)
    pick = pick.astype(BF)
    pick_out[...] = pick
    weigh_out[...] = weighted.astype(BF)
    out[...] = mm(pick, x[:, : out.shape[1]], NN).astype(BF)


def rest_body(at, pick, weighted, x, dy, *outs):
    for chosen, source, pieces in zip((pick, weighted), (x, dy), plan(x.shape[1])):
        for message, column, feature, many in pieces:
            if message > 0:
                value = mm(chosen[...], source[:, feature : feature + many], NN)
                outs[message - 1][:, column : column + many] = value.astype(BF)


def halves_body(at, gate, up, down, out, token):
    token[...] = jnp.zeros((8, 128), F32)
    units, block = down.shape
    out[0, 0] = gate[...]
    out[0, 1] = up[...]
    for j in range(0, block, units):
        out[0, 2, j : j + units, :] = down[:, j : j + units]


def halves(at, w_gate, w_up, w_down):
    depth, units = w_gate.shape
    block = depth // (2 * CHIPS)
    other = lambda r, at: 2 * ((at[0] + r) % CHIPS) + 1 - at[1]
    tall = pl.BlockSpec((block, units), lambda r, at: (other(r, at), 0))
    wide = pl.BlockSpec((units, block), lambda r, at: (0, other(r, at)))
    return pl.pallas_call(
        halves_body,
        out_shape=(shape((CHIPS, 3, block, units), BF), shape((8, 128), F32)),
        compiler_params=pltpu.CompilerParams(vmem_limit_bytes=VMEM_LIMIT),
        cost_estimate=pl.CostEstimate(flops=0, bytes_accessed=12 * depth * units, transcendentals=0),
        grid_spec=pltpu.PrefetchScalarGridSpec(
            num_scalar_prefetch=1,
            grid=(CHIPS,),
            in_specs=[tall, tall, wide],
            out_specs=[
                pl.BlockSpec((1, 3, block, units), lambda r, at: (r, 0, 0, 0)),
                pl.BlockSpec((8, 128), lambda r, at: (0, 0)),
            ],
        ),
    )(at, w_gate, w_up, w_down)


def block_at(at, r):
    return 2 * lax.rem(at[0] + r, CHIPS) + at[1]


def pre_weights(at, gate, up, others, r, lo, hi):
    block = others.shape[2]
    mine = pl.ds(pl.multiple_of(block_at(at, r) * block + lo, 128), hi - lo)
    return jnp.concatenate([gate[mine, :], others[r, 0, lo:hi, :], up[mine, :], others[r, 1, lo:hi, :]], axis=1)


def down_weights(at, down, others, r, lo, hi):
    units = down.shape[0]
    block = others.shape[2]
    mine = pl.ds(pl.multiple_of(block_at(at, r) * block + lo, 128), hi - lo)
    other = [others[r, 2, j : j + units, :] for j in range(lo, hi, units)]
    return jnp.concatenate([down[:, mine], jnp.concatenate(other, axis=1)], axis=0)


def halves_of(parts, r, half, columns):
    if r == 2:
        return ((0, parts[3][:, columns]), (half, parts[4][:, columns]))
    ref = parts[{0: 0, 1: 1, 3: 2}[r]]
    return ((0, ref[:half, columns]), (half, ref[half:, columns]))


def swapped(value, units):
    pieces = [value[:, i : i + units] for i in range(0, value.shape[1], units)]
    return jnp.concatenate([pieces[i ^ 1] for i in range(len(pieces))], axis=1).astype(BF)


def add_body(piece, which, first, pre, at, *refs):
    _, column, feature, many = piece
    columns = slice(column, column + many)
    weights, refs = (refs[:3], refs[3:]) if pre else (refs[:2], refs[2:])
    given = 3 * (which[0] == 0) + 2 * (2 in which)
    parts, refs = refs[:given], refs[given:]
    parts = [None] * (5 - given) + list(parts) if which[0] == 2 else parts
    before, refs = (None, refs) if first else (refs[0], refs[1:])
    keep = refs[0]
    half = keep.shape[0] // 2
    for r in which:
        cut = (feature, feature + many)
        block = pre_weights(at, *weights, r, *cut) if pre else down_weights(at, *weights, r, *cut)
        for lo, part in halves_of(parts, r, half, columns):
            value = mm(part, block, NN if pre else NT)
            if r == which[0]:
                keep[lo : lo + half, :] = value if first else before[lo : lo + half, :] + value
            else:
                keep[lo : lo + half, :] += value


def split_body(at, left, right, out_a, out_b):
    half = left.shape[0] // 2
    out_a[...] = left[:half, :]
    out_b[...] = right[half:, :]


def turn_body(piece, at, own, right, left, gate, up, others, out_a, out_b, pre):
    split_body(at, left, right, out_a, out_b)
    add_body(piece, (0, 1, 3), True, True, at, gate, up, others, own, right, left, pre)


def early_body(x_piece, dy_piece, at, gate, up, others, down, *refs):
    far, before, dy, (pre, back) = refs[:2], refs[2], refs[3:6], refs[6:]
    add_body(x_piece, (2,), False, True, at, gate, up, others, *far, before, pre)
    add_body(dy_piece, (0, 1, 3), True, False, at, down, others, *dy, back)


def late_body(dy_piece, at, down, others, opp_a, opp_b, before, pre, back, send):
    add_body(dy_piece, (2,), False, False, at, down, others, opp_a, opp_b, before, back)
    units = down.shape[0]
    send[:, : 4 * units] = swapped(pre[...], units)
    send[:, 4 * units :] = swapped(back[...], units)


def middle_body(at, pre, back, recv, gate, up, others, d, act_rows, sums, opp_a, opp_b):
    rows = pre.shape[0]
    both = pre.shape[1] // 2
    half = rows // 2
    experts = rows // CAP
    owner = owner_of(rows, experts)
    slot = slot_is(rows, CAP)
    weights = pre_weights(at, gate, up, others, 2, 0, opp_a.shape[1])
    total = None
    for lo, out in ((0, opp_a), (half, opp_b)):
        span = slice(lo, lo + half)
        pre_all = pre[span, :] + recv[span, : 2 * both].astype(F32)
        back_all = back[span, :] + recv[span, 2 * both :].astype(F32)
        pre_gate = pre_all[:, :both]
        pre_up = pre_all[:, both:]
        sig = jax.nn.sigmoid(pre_gate)
        silu = pre_gate * sig
        act = silu * pre_up
        act_rows[span, :] = act.astype(BF)
        d_gate = (back_all * pre_up * (sig * (1.0 + pre_gate * (1.0 - sig)))).astype(BF)
        d_up = (back_all * silu).astype(BF)
        grads = jnp.concatenate([d_gate, d_up], axis=1)
        d[span, :] = grads
        out[...] = mm(grads, weights, NT).astype(BF)
        value = jnp.sum(act * back_all, axis=1, keepdims=True)
        part = lax.dot_general(
            owner[span, :],
            jnp.where(slot[span, :], value, 0.0),
            TN,
            preferred_element_type=F32,
            precision=lax.Precision.HIGHEST,
        )
        total = part if total is None else total + part
    sums[...] = total


def rows_body(at, d, gate, up, others, to_right, to_left, right_later, left_later, own):
    half = d.shape[0] // 2
    block = own.shape[1]
    weights = pre_weights(at, gate, up, others, 1, 0, block)
    to_right[...] = mm(d[half:, :], weights, NT).astype(BF)
    right_later[...] = mm(d[:half, :], weights, NT)
    weights = pre_weights(at, gate, up, others, 3, 0, block)
    to_left[...] = mm(d[:half, :], weights, NT).astype(BF)
    left_later[...] = mm(d[half:, :], weights, NT)
    weights = pre_weights(at, gate, up, others, 0, 0, block)
    own[:half, :] = mm(d[:half, :], weights, NT)
    own[half:, :] = mm(d[half:, :], weights, NT)


def later_body(at, right_later, left_later, from_left, from_right, to_right, to_left):
    to_right[...] = (right_later[...] + from_left[...].astype(F32)).astype(BF)
    to_left[...] = (left_later[...] + from_right[...].astype(F32)).astype(BF)


def total_body(at, own, left_a, left_b, right_a, right_b, out):
    half = own.shape[0] // 2
    for span, left, right in ((slice(0, half), left_a, right_a), (slice(half, 2 * half), left_b, right_b)):
        out[span, :] = (own[span, :] + left[...].astype(F32) + right[...].astype(F32)).astype(BF)


def grads_body(at, d, act_rows, *refs):
    keep, send = refs[-2:]
    messages = [refs[i : i + 5] for i in range(0, len(refs) - 2, 5)]
    block = keep.shape[2]
    units = keep.shape[3]
    half = d.shape[0] // 2
    tokens, cotangents = plan(block)
    for r in range(CHIPS):
        for message, column, feature, many in tokens:
            total = None
            for lo, part in halves_of(messages[message], r, half, slice(column, column + many)):
                value = mm(part, d[lo : lo + half, :], TN)
                total = value if total is None else total + value
            for i, (out, kind) in enumerate(((keep, 0), (send, 0), (keep, 1), (send, 1))):
                out[r, kind, feature : feature + many, :] = total[:, i * units : (i + 1) * units].astype(BF)
        for message, column, feature, many in cotangents:
            total = None
            for lo, part in halves_of(messages[message], r, half, slice(column, column + many)):
                value = mm(act_rows[lo : lo + half, :], part, TN)
                total = value if total is None else total + value
            total = total.astype(BF)
            for j in range(0, many, units):
                keep[r, 2, feature + j : feature + j + units, :] = total[:units, j : j + units]
                send[r, 2, feature + j : feature + j + units, :] = total[units:, j : j + units]


def place_body(at, keep, recv, gate, up, down, token):
    token[...] = jnp.zeros((8, 128), F32)
    units = gate.shape[1]
    mine = lax.rem(pl.program_id(0), 2) == at[1]

    def put(held):
        gate[...] = held[0, 0]
        up[...] = held[0, 1]
        for j in range(0, gate.shape[0], units):
            down[:, j : j + units] = held[0, 2, j : j + units, :]

    @pl.when(mine)
    def _():
        put(keep)

    @pl.when(jnp.logical_not(mine))
    def _():
        put(recv)


def place(at, keep, recv):
    _, _, block, units = keep.shape
    depth = 2 * CHIPS * block
    source = pl.BlockSpec((1, 3, block, units), lambda b, at: ((b // 2 + CHIPS - at[0]) % CHIPS, 0, 0, 0))
    return pl.pallas_call(
        place_body,
        out_shape=(
            shape((depth, units), BF),
            shape((depth, units), BF),
            shape((units, depth), BF),
            shape((8, 128), F32),
        ),
        compiler_params=pltpu.CompilerParams(vmem_limit_bytes=VMEM_LIMIT),
        cost_estimate=pl.CostEstimate(flops=0, bytes_accessed=12 * depth * units, transcendentals=0),
        grid_spec=pltpu.PrefetchScalarGridSpec(
            num_scalar_prefetch=1,
            grid=(2 * CHIPS,),
            in_specs=[source, source],
            out_specs=[
                pl.BlockSpec((block, units), lambda b, at: (b, 0)),
                pl.BlockSpec((block, units), lambda b, at: (b, 0)),
                pl.BlockSpec((units, block), lambda b, at: (0, b)),
                pl.BlockSpec((8, 128), lambda b, at: (0, 0)),
            ],
        ),
    )(at, keep, recv)


def finish_body(at, pick, back, grad):
    grad[...] = mm(pick[...], back[...], TN).astype(BF)


def gating_body(at, pick, routes, gates, sums, left, far, right, grad):
    topk, count = routes.shape
    rows = pick.shape[0]
    experts = rows // CAP
    owner = owner_of(rows, experts)
    spread = lax.dot_general(
        owner, sums[...] + left[...] + far[...] + right[...], NN, preferred_element_type=F32, precision=lax.Precision.HIGHEST
    )
    value = jnp.sum(jnp.where(slot_is(rows, CAP), spread, 0.0), axis=1, keepdims=True)
    table = lax.dot_general(
        owner, pick[...].astype(F32) * value, TN, preferred_element_type=F32, precision=lax.Precision.HIGHEST
    )
    expert = lax.broadcasted_iota(jnp.int32, (experts, count), 0)
    for k in range(topk):
        hit = routes[k : k + 1, :] == expert
        picked = jnp.sum(jnp.where(hit, table, 0.0), axis=0, keepdims=True)
        grad[k : k + 1, :] = picked / gates[k : k + 1, :].astype(F32)


def to(value, shift):
    size = 2 * CHIPS
    return lax.ppermute(value, "hidden", [(i, (i + 2 * shift) % size) for i in range(size)])


def swap(value):
    return lax.ppermute(value, "hidden", [(i, i ^ 1) for i in range(2 * CHIPS)])


def behind(value, token):
    return pl.pallas_call(
        lambda *refs: None,
        out_shape=shape(value.shape, value.dtype),
        in_specs=[ANY, ANY],
        out_specs=ANY,
        input_output_aliases={0: 0},
        compiler_params=pltpu.CompilerParams(vmem_limit_bytes=VMEM_LIMIT // 4),
    )(value, token)


def local(tokens, grad_out, routes, gating, w_gate, w_up, w_down):
    experts = lax.axis_size("expert")
    hidden = lax.axis_index("hidden")
    at = jnp.stack([lax.shift_right_logical(hidden, 1), lax.bitwise_and(hidden, 1)]).astype(jnp.int32)
    rows = experts * CAP
    half = rows // 2
    count, width = tokens.shape
    topk = routes.shape[1]
    block = width // (2 * CHIPS)
    gate, up, down = w_gate[0], w_up[0], w_down[0]
    units = gate.shape[1]
    both = 2 * units
    routes, gates = routes.T, gating.T
    of_tokens, of_cotangents = plan(block)

    def over_experts(value):
        split = value.reshape(experts, value.shape[0] // experts, value.shape[1])
        return lax.all_to_all(split, "expert", split_axis=0, concat_axis=0, tiled=True).reshape(value.shape)

    def my_block(value):
        return lax.dynamic_slice(value, (0, hidden * block), (count, block))

    my_tokens = my_block(tokens)
    message, pick, weighted = call(
        functools.partial(first_body, experts),
        (shape((rows, widths(block)[0]), BF),) + (shape((rows, count), BF),) * 2,
        (at, routes, gates, my_tokens),
    )
    arrived = [over_experts(message)]
    halved, token = halves(at, gate, up, down)
    messages = call(
        rest_body,
        tuple(shape((rows, many), BF) for many in widths(block)[1:]),
        (at, pick, weighted, my_tokens, my_block(grad_out)),
        after=(token,),
    )
    arrived += [over_experts(message) for message in messages]
    others = swap(halved)
    weights = (gate, up, others)
    (x_piece,), (dy_piece,) = of_tokens, of_cotangents
    part = (shape((half, block), BF),)

    left, right = to(arrived[0], 1), to(arrived[0], -1)
    pass_a, pass_b, pre, *token = call(
        functools.partial(turn_body, x_piece),
        part * 2 + (shape((rows, 2 * both), F32),),
        (at, arrived[0], right, left, *weights),
        token=True,
    )
    x = (arrived[0], right, left, to(pass_a, 1), to(pass_b, -1))
    left, right = to(arrived[1], 1), to(arrived[1], -1)
    pass_a, pass_b, *token = call(split_body, part * 2, (at, left, right), after=token, token=True)
    dy = (arrived[1], right, left, to(pass_a, 1), to(pass_b, -1))

    narrow = shape((rows, both), F32)
    pre, back = call(
        functools.partial(early_body, x_piece, dy_piece),
        (shape((rows, 2 * both), F32), narrow),
        (at, *weights, down, *x[3:], pre, *dy[:3]),
        after=token,
    )
    back, send = call(
        functools.partial(late_body, dy_piece),
        (narrow, shape((rows, 3 * both), BF)),
        (at, down, others, *dy[3:], back, pre),
    )
    recv = swap(send)

    later = (shape((half, block), F32),)
    d, act_rows, sums, opp_a, opp_b = call(
        middle_body,
        (shape((rows, 2 * both), BF), shape((rows, both), BF), shape((experts, CAP), F32)) + part * 2,
        (at, pre, back, recv, *weights),
    )
    from_left, from_right = to(opp_a, 1), to(opp_b, -1)
    to_right, to_left, right_later, left_later, own, *token = call(
        rows_body,
        part * 2 + later * 2 + (shape((rows, block), F32),),
        (at, d, *weights),
        token=True,
    )
    left_b, right_a = to(to_right, 1), to(to_left, -1)
    keep, send, *token = call(
        grads_body,
        (shape((CHIPS, 3, block, units), BF),) * 2,
        (at, d, act_rows, *x, *dy),
        after=token,
        token=True,
    )
    to_right, to_left = call(later_body, part * 2, (at, right_later, left_later, from_left, from_right), after=token)
    left_a, right_b = to(to_right, 1), to(to_left, -1)
    slots = over_experts(sums)
    total, *token = call(
        total_body,
        (shape((rows, block), BF),),
        (at, own, left_a, left_b, right_a, right_b),
        after=(slots,),
        token=True,
    )
    returned = over_experts(total)
    *grads, placed = place(at, keep, swap(behind(send, token[0])))
    grad_gating, gated = call(
        gating_body,
        (shape((topk, count), F32),),
        (at, pick, routes, gates, slots, *[to(slots, shift) for shift in (1, 2, 3)]),
        token=True,
    )
    (grad_tokens,) = call(
        finish_body,
        (shape((count, block), BF),),
        (at, pick, returned),
        after=(gated, placed),
    )
    return (grad_tokens, grad_gating.T, grads[0][None], grads[1][None], grads[2][None])


def solution(mesh):
    placed = (
        P("expert", None),
        P("expert", None),
        P("expert", None),
        P("expert", None),
        P("expert", None, "hidden"),
        P("expert", None, "hidden"),
        P("expert", "hidden", None),
    )
    return jax.shard_map(
        local,
        mesh=mesh,
        in_specs=placed,
        out_specs=(
            P("expert", "hidden"),
            P("expert", None),
            P("expert", None, "hidden"),
            P("expert", None, "hidden"),
            P("expert", "hidden", None),
        ),
        check_vma=False,
    )
```

```python
import functools

import jax
import jax.numpy as jnp
from jax import lax
from jax.experimental import pallas as pl
from jax.experimental.pallas import tpu as pltpu
from jax.sharding import PartitionSpec as P

CAP = 16
CHIPS = 4
BF = jnp.bfloat16
F32 = jnp.float32
VMEM_LIMIT = 16 * 1024 * 1024


NN = (((1,), (0,)), ((), ()))
NT = (((1,), (1,)), ((), ()))
TN = (((0,), (0,)), ((), ()))


def mm(a, b, dims):
    return lax.dot_general(a, b, dims, preferred_element_type=F32)


def call(body, out_shape, operands, after=(), token=False, scratch=(), places=None, outs=None):
    count = len(operands)
    out_shape = tuple(out_shape)
    results = len(out_shape)
    ins = places or [SM] + [VM] * (count - 1)
    outs = outs or (VM,) * results

    moved = sum(v.size * v.dtype.itemsize for v in tuple(operands[1:]) + out_shape)

    def run(*refs):
        given, made = refs[:count], refs[count + len(after) :]
        if token:
            made[results][...] = jnp.zeros((8, 128), F32)
            made = made[:results] + made[results + 1 :]
        body(*given, *made)

    return pl.pallas_call(
        run,
        out_shape=out_shape + ((shape((8, 128), F32),) if token else ()),
        in_specs=list(ins) + [ANY] * len(after),
        out_specs=tuple(outs) + ((VM,) if token else ()),
        scratch_shapes=list(scratch),
        compiler_params=pltpu.CompilerParams(vmem_limit_bytes=VMEM_LIMIT),
        cost_estimate=pl.CostEstimate(flops=0, bytes_accessed=moved, transcendentals=0),
    )(*operands, *after)


def shape(dims, dtype):
    return jax.ShapeDtypeStruct(dims, dtype)


VM = pl.BlockSpec(memory_space=pltpu.VMEM)
SM = pl.BlockSpec(memory_space=pltpu.SMEM)
ANY = pl.BlockSpec(memory_space=pl.ANY)


def owner_of(rows, experts):
    row = lax.broadcasted_iota(jnp.int32, (rows, experts), 0) // CAP
    return (row == lax.broadcasted_iota(jnp.int32, (rows, experts), 1)).astype(F32)


def slot_is(rows, count):
    row = lax.broadcasted_iota(jnp.int32, (rows, count), 0) % CAP
    return row == lax.broadcasted_iota(jnp.int32, (rows, count), 1)


def select_rows(routes, rows, experts):
    topk, count = routes.shape
    expert = lax.broadcasted_iota(jnp.int32, (experts, count), 0)
    named = jnp.zeros((experts, count), F32)
    for k in range(topk):
        named = jnp.where(routes[k : k + 1, :] == expert, 1.0, named)
    earlier = (
        lax.broadcasted_iota(jnp.int32, (count, count), 0) < lax.broadcasted_iota(jnp.int32, (count, count), 1)
    ).astype(F32)
    slot = mm(named.astype(BF), earlier.astype(BF), NN)
    slot = jnp.where(named > 0, slot, 2.0 * CAP)
    owner = owner_of(rows, experts).astype(BF)
    slot_of = mm(owner, slot.astype(BF), NN)
    place = (lax.broadcasted_iota(jnp.int32, (rows, count), 0) % CAP).astype(F32)
    return jnp.where(slot_of == place, 1.0, 0.0)


def weigh_rows(pick, routes, gates):
    topk, count = routes.shape
    rows = pick.shape[0]
    experts = rows // CAP
    expert = lax.broadcasted_iota(jnp.int32, (experts, count), 0)
    weight = jnp.zeros((experts, count), F32)
    for k in range(topk):
        weight = jnp.where(routes[k : k + 1, :] == expert, gates[k : k + 1, :].astype(F32), weight)
    return pick.astype(F32) * mm(owner_of(rows, experts).astype(BF), weight.astype(BF), NN)


def first_body(experts, at, routes, x, out, pick_out):
    pick = select_rows(routes[...], pick_out.shape[0], experts).astype(BF)
    pick_out[...] = pick
    out[...] = mm(pick, x[...], NN).astype(BF)


def rest_body(at, pick, routes, gates, dy, out):
    weighted = weigh_rows(pick[...], routes[...], gates[...]).astype(BF)
    out[...] = mm(weighted, dy[...], NN).astype(BF)


def halves_body(at, gate, up, down, out, token):
    token[...] = jnp.zeros((8, 128), F32)
    units, block = down.shape
    out[0, 0] = gate[...]
    out[0, 1] = up[...]
    for j in range(0, block, units):
        out[0, 2, j : j + units, :] = down[:, j : j + units]


def halves(at, w_gate, w_up, w_down):
    depth, units = w_gate.shape
    block = depth // (2 * CHIPS)
    other = lambda r, at: 2 * ((at[0] + r) % CHIPS) + 1 - at[1]
    tall = pl.BlockSpec((block, units), lambda r, at: (other(r, at), 0))
    wide = pl.BlockSpec((units, block), lambda r, at: (0, other(r, at)))
    return pl.pallas_call(
        halves_body,
        out_shape=(shape((CHIPS, 3, block, units), BF), shape((8, 128), F32)),
        compiler_params=pltpu.CompilerParams(vmem_limit_bytes=VMEM_LIMIT),
        cost_estimate=pl.CostEstimate(flops=0, bytes_accessed=12 * depth * units, transcendentals=0),
        grid_spec=pltpu.PrefetchScalarGridSpec(
            num_scalar_prefetch=1,
            grid=(CHIPS,),
            in_specs=[tall, tall, wide],
            out_specs=[
                pl.BlockSpec((1, 3, block, units), lambda r, at: (r, 0, 0, 0)),
                pl.BlockSpec((8, 128), lambda r, at: (0, 0)),
            ],
        ),
    )(at, w_gate, w_up, w_down)


def block_at(at, r):
    return 2 * lax.rem(at[0] + r, CHIPS) + at[1]


def pre_weights(at, gate, up, others, r, lo, hi):
    block = others.shape[2]
    mine = pl.ds(pl.multiple_of(block_at(at, r) * block + lo, 128), hi - lo)
    return jnp.concatenate([gate[mine, :], others[r, 0, lo:hi, :], up[mine, :], others[r, 1, lo:hi, :]], axis=1)


def down_weights(at, down, others, r, lo, hi):
    units = down.shape[0]
    block = others.shape[2]
    mine = pl.ds(pl.multiple_of(block_at(at, r) * block + lo, 128), hi - lo)
    other = [others[r, 2, j : j + units, :] for j in range(lo, hi, units)]
    return jnp.concatenate([down[:, mine], jnp.concatenate(other, axis=1)], axis=0)


def halves_of(parts, r, half):
    if r == 2:
        return ((0, parts[3][...]), (half, parts[4][...]))
    ref = parts[{0: 0, 1: 1, 3: 2}[r]]
    return ((0, ref[:half, :]), (half, ref[half:, :]))


def swapped(value, units):
    pieces = [value[:, i : i + units] for i in range(0, value.shape[1], units)]
    return jnp.concatenate([pieces[i ^ 1] for i in range(len(pieces))], axis=1).astype(BF)


def add_body(which, first, pre, at, *refs):
    weights, refs = (refs[:3], refs[3:]) if pre else (refs[:2], refs[2:])
    given = 3 * (which[0] == 0) + 2 * (2 in which)
    parts, refs = refs[:given], refs[given:]
    parts = [None] * (5 - given) + list(parts) if which[0] == 2 else parts
    before, refs = (None, refs) if first else (refs[0], refs[1:])
    keep = refs[0]
    half = keep.shape[0] // 2
    for r in which:
        width = weights[-1].shape[2]
        block = pre_weights(at, *weights, r, 0, width) if pre else down_weights(at, *weights, r, 0, width)
        for lo, part in halves_of(parts, r, half):
            value = mm(part, block, NN if pre else NT)
            if r == which[0]:
                keep[lo : lo + half, :] = value if first else before[lo : lo + half, :] + value
            else:
                keep[lo : lo + half, :] += value


def split_body(at, left, right, out_a, out_b):
    half = left.shape[0] // 2
    out_a[...] = left[:half, :]
    out_b[...] = right[half:, :]


def turn_body(at, own, right, left, gate, up, others, out_a, out_b, pre):
    split_body(at, left, right, out_a, out_b)
    add_body((0, 1, 3), True, True, at, gate, up, others, own, right, left, pre)


def early_body(at, gate, up, others, down, *refs):
    far, before, dy, (pre, back, pre_send) = refs[:2], refs[2], refs[3:6], refs[6:]
    add_body((2,), False, True, at, gate, up, others, *far, before, pre)
    pre_send[...] = swapped(pre[...], down.shape[0])
    add_body((0, 1, 3), True, False, at, down, others, *dy, back)


def late_body(at, down, others, opp_a, opp_b, before, pre_send, back, send):
    add_body((2,), False, False, at, down, others, opp_a, opp_b, before, back)
    units = down.shape[0]
    send[:, : 4 * units] = pre_send[...]
    send[:, 4 * units :] = swapped(back[...], units)


def middle_body(at, pre, back, recv, gate, up, others, d, act_rows, values, opp_a, opp_b):
    rows = pre.shape[0]
    both = pre.shape[1] // 2
    half = rows // 2
    weights = pre_weights(at, gate, up, others, 2, 0, opp_a.shape[1])
    for lo, out in ((0, opp_a), (half, opp_b)):
        span = slice(lo, lo + half)
        pre_all = pre[span, :] + recv[span, : 2 * both].astype(F32)
        back_all = back[span, :] + recv[span, 2 * both :].astype(F32)
        pre_gate = pre_all[:, :both]
        pre_up = pre_all[:, both:]
        sig = jax.nn.sigmoid(pre_gate)
        silu = pre_gate * sig
        act = silu * pre_up
        act_rows[span, :] = act.astype(BF)
        d_gate = (back_all * pre_up * (sig * (1.0 + pre_gate * (1.0 - sig)))).astype(BF)
        d_up = (back_all * silu).astype(BF)
        grads = jnp.concatenate([d_gate, d_up], axis=1)
        d[span, :] = grads
        out[...] = mm(grads, weights, NT).astype(BF)
        value = jnp.sum(act * back_all, axis=1, keepdims=True)
        values[span, :] = jnp.broadcast_to(value, (half, values.shape[1]))


def rows_body(at, d, values, gate, up, others, to_right, to_left, right_later, left_later, own, sums):
    half = d.shape[0] // 2
    block = own.shape[1]
    weights = pre_weights(at, gate, up, others, 1, 0, block)
    to_right[...] = mm(d[half:, :], weights, NT).astype(BF)
    right_later[...] = mm(d[:half, :], weights, NT)
    weights = pre_weights(at, gate, up, others, 3, 0, block)
    to_left[...] = mm(d[:half, :], weights, NT).astype(BF)
    left_later[...] = mm(d[half:, :], weights, NT)
    weights = pre_weights(at, gate, up, others, 0, 0, block)
    own[:half, :] = mm(d[:half, :], weights, NT)
    own[half:, :] = mm(d[half:, :], weights, NT)
    rows = d.shape[0]
    sums[...] = lax.dot_general(
        owner_of(rows, rows // CAP),
        jnp.where(slot_is(rows, CAP), values[:, :CAP], 0.0),
        TN,
        preferred_element_type=F32,
        precision=lax.Precision.HIGHEST,
    )


def later_body(at, right_later, left_later, from_left, from_right, to_right, to_left):
    to_right[...] = (right_later[...] + from_left[...].astype(F32)).astype(BF)
    to_left[...] = (left_later[...] + from_right[...].astype(F32)).astype(BF)


def total_body(at, own, left_a, left_b, right_a, right_b, out):
    half = own.shape[0] // 2
    for span, left, right in ((slice(0, half), left_a, right_a), (slice(half, 2 * half), left_b, right_b)):
        out[span, :] = (own[span, :] + left[...].astype(F32) + right[...].astype(F32)).astype(BF)


def grads_body(at, d, act_rows, *refs):
    x, dy, (keep, send) = refs[:5], refs[5:10], refs[10:]
    block, units = keep.shape[2:]
    half = d.shape[0] // 2
    for r in range(CHIPS):
        total = None
        for lo, part in halves_of(x, r, half):
            value = mm(part, d[lo : lo + half, :], TN)
            total = value if total is None else total + value
        for i, (out, kind) in enumerate(((keep, 0), (send, 0), (keep, 1), (send, 1))):
            out[r, kind] = total[:, i * units : (i + 1) * units].astype(BF)
        total = None
        for lo, part in halves_of(dy, r, half):
            value = mm(act_rows[lo : lo + half, :], part, TN)
            total = value if total is None else total + value
        total = total.astype(BF)
        for j in range(0, block, units):
            keep[r, 2, j : j + units, :] = total[:units, j : j + units]
            send[r, 2, j : j + units, :] = total[units:, j : j + units]


def place_body(at, keep, recv, gate, up, down, token):
    token[...] = jnp.zeros((8, 128), F32)
    units = gate.shape[1]
    mine = lax.rem(pl.program_id(0), 2) == at[1]

    def put(held):
        gate[...] = held[0, 0]
        up[...] = held[0, 1]
        for j in range(0, gate.shape[0], units):
            down[:, j : j + units] = held[0, 2, j : j + units, :]

    @pl.when(mine)
    def _():
        put(keep)

    @pl.when(jnp.logical_not(mine))
    def _():
        put(recv)


def place(at, keep, recv):
    _, _, block, units = keep.shape
    depth = 2 * CHIPS * block
    source = pl.BlockSpec((1, 3, block, units), lambda b, at: ((b // 2 + CHIPS - at[0]) % CHIPS, 0, 0, 0))
    return pl.pallas_call(
        place_body,
        out_shape=(
            shape((depth, units), BF),
            shape((depth, units), BF),
            shape((units, depth), BF),
            shape((8, 128), F32),
        ),
        compiler_params=pltpu.CompilerParams(vmem_limit_bytes=VMEM_LIMIT),
        cost_estimate=pl.CostEstimate(flops=0, bytes_accessed=12 * depth * units, transcendentals=0),
        grid_spec=pltpu.PrefetchScalarGridSpec(
            num_scalar_prefetch=1,
            grid=(2 * CHIPS,),
            in_specs=[source, source],
            out_specs=[
                pl.BlockSpec((block, units), lambda b, at: (b, 0)),
                pl.BlockSpec((block, units), lambda b, at: (b, 0)),
                pl.BlockSpec((units, block), lambda b, at: (0, b)),
                pl.BlockSpec((8, 128), lambda b, at: (0, 0)),
            ],
        ),
    )(at, keep, recv)


def finish_body(at, pick, back, grad):
    grad[...] = mm(pick[...], back[...], TN).astype(BF)


def gating_body(at, pick, routes, gates, sums, left, far, right, grad):
    topk, count = routes.shape
    rows = pick.shape[0]
    experts = rows // CAP
    owner = owner_of(rows, experts)
    spread = lax.dot_general(
        owner, sums[...] + left[...] + far[...] + right[...], NN, preferred_element_type=F32, precision=lax.Precision.HIGHEST
    )
    value = jnp.sum(jnp.where(slot_is(rows, CAP), spread, 0.0), axis=1, keepdims=True)
    table = lax.dot_general(
        owner, pick[...].astype(F32) * value, TN, preferred_element_type=F32, precision=lax.Precision.HIGHEST
    )
    expert = lax.broadcasted_iota(jnp.int32, (experts, count), 0)
    for k in range(topk):
        hit = routes[k : k + 1, :] == expert
        picked = jnp.sum(jnp.where(hit, table, 0.0), axis=0, keepdims=True)
        grad[k : k + 1, :] = picked / gates[k : k + 1, :].astype(F32)


def to(value, shift):
    size = 2 * CHIPS
    return lax.ppermute(value, "hidden", [(i, (i + 2 * shift) % size) for i in range(size)])


def swap(value):
    return lax.ppermute(value, "hidden", [(i, i ^ 1) for i in range(2 * CHIPS)])


def behind(value, token):
    return pl.pallas_call(
        lambda *refs: None,
        out_shape=shape(value.shape, value.dtype),
        in_specs=[ANY, ANY],
        out_specs=ANY,
        input_output_aliases={0: 0},
        compiler_params=pltpu.CompilerParams(vmem_limit_bytes=VMEM_LIMIT // 4),
    )(value, token)


def local(tokens, grad_out, routes, gating, w_gate, w_up, w_down):
    experts = lax.axis_size("expert")
    hidden = lax.axis_index("hidden")
    at = jnp.stack([lax.shift_right_logical(hidden, 1), lax.bitwise_and(hidden, 1)]).astype(jnp.int32)
    rows = experts * CAP
    half = rows // 2
    count, width = tokens.shape
    topk = routes.shape[1]
    block = width // (2 * CHIPS)
    gate, up, down = w_gate[0], w_up[0], w_down[0]
    units = gate.shape[1]
    both = 2 * units
    routes, gates = routes.T, gating.T

    def over_experts(value):
        split = value.reshape(experts, value.shape[0] // experts, value.shape[1])
        return lax.all_to_all(split, "expert", split_axis=0, concat_axis=0, tiled=True).reshape(value.shape)

    def my_block(value):
        return lax.dynamic_slice(value, (0, hidden * block), (count, block))

    message, pick = call(
        functools.partial(first_body, experts),
        (shape((rows, block), BF), shape((rows, count), BF)),
        (at, routes, my_block(tokens)),
    )
    arrived = [over_experts(message)]
    halved, token = halves(at, gate, up, down)
    (message,) = call(
        rest_body, (shape((rows, block), BF),), (at, pick, routes, gates, my_block(grad_out)), after=(token,)
    )
    arrived.append(over_experts(message))
    others = swap(halved)
    weights = (gate, up, others)
    part = (shape((half, block), BF),)

    left, right = to(arrived[0], 1), to(arrived[0], -1)
    pass_a, pass_b, pre, *token = call(
        turn_body,
        part * 2 + (shape((rows, 2 * both), F32),),
        (at, arrived[0], right, left, *weights),
        token=True,
    )
    x = (arrived[0], right, left, to(pass_a, 1), to(pass_b, -1))
    left, right = to(arrived[1], 1), to(arrived[1], -1)
    pass_a, pass_b, *token = call(split_body, part * 2, (at, left, right), after=token, token=True)
    dy = (arrived[1], right, left, to(pass_a, 1), to(pass_b, -1))

    narrow = shape((rows, both), F32)
    pre, back, pre_send = call(
        early_body,
        (shape((rows, 2 * both), F32), narrow, shape((rows, 2 * both), BF)),
        (at, *weights, down, *x[3:], pre, *dy[:3]),
        after=token,
    )
    back, send = call(
        late_body,
        (narrow, shape((rows, 3 * both), BF)),
        (at, down, others, *dy[3:], back, pre_send),
    )
    recv = swap(send)

    later = (shape((half, block), F32),)
    d, act_rows, values, opp_a, opp_b = call(
        middle_body,
        (shape((rows, 2 * both), BF), shape((rows, both), BF), shape((rows, 128), F32)) + part * 2,
        (at, pre, back, recv, *weights),
    )
    from_left, from_right = to(opp_a, 1), to(opp_b, -1)
    to_right, to_left, right_later, left_later, own, sums, *token = call(
        rows_body,
        part * 2 + later * 2 + (shape((rows, block), F32), shape((experts, CAP), F32)),
        (at, d, values, *weights),
        token=True,
    )
    left_b, right_a = to(to_right, 1), to(to_left, -1)
    keep, send, *token = call(
        grads_body,
        (shape((CHIPS, 3, block, units), BF),) * 2,
        (at, d, act_rows, *x, *dy),
        after=token,
        token=True,
    )
    to_right, to_left = call(later_body, part * 2, (at, right_later, left_later, from_left, from_right), after=token)
    left_a, right_b = to(to_right, 1), to(to_left, -1)
    slots = over_experts(sums)
    total, *token = call(
        total_body,
        (shape((rows, block), BF),),
        (at, own, left_a, left_b, right_a, right_b),
        after=(slots,),
        token=True,
    )
    returned = over_experts(total)
    *grads, placed = place(at, keep, swap(behind(send, token[0])))
    grad_gating, gated = call(
        gating_body,
        (shape((topk, count), F32),),
        (at, pick, routes, gates, slots, *[to(slots, shift) for shift in (1, 2, 3)]),
        token=True,
    )
    (grad_tokens,) = call(
        finish_body,
        (shape((count, block), BF),),
        (at, pick, returned),
        after=(gated, placed),
    )
    return (grad_tokens, grad_gating.T, grads[0][None], grads[1][None], grads[2][None])


def solution(mesh):
    placed = (
        P("expert", None),
        P("expert", None),
        P("expert", None),
        P("expert", None),
        P("expert", None, "hidden"),
        P("expert", None, "hidden"),
        P("expert", "hidden", None),
    )
    return jax.shard_map(
        local,
        mesh=mesh,
        in_specs=placed,
        out_specs=(
            P("expert", "hidden"),
            P("expert", None),
            P("expert", None, "hidden"),
            P("expert", None, "hidden"),
            P("expert", "hidden", None),
        ),
        check_vma=False,
    )
```

```python
import functools

import jax
import jax.numpy as jnp
from jax import lax
from jax.experimental import pallas as pl
from jax.experimental.pallas import tpu as pltpu
from jax.sharding import PartitionSpec as P

CAP = 16
CHIPS = 4
BF = jnp.bfloat16
F32 = jnp.float32
VMEM_LIMIT = 16 * 1024 * 1024


NN = (((1,), (0,)), ((), ()))
NT = (((1,), (1,)), ((), ()))
TN = (((0,), (0,)), ((), ()))


def mm(a, b, dims):
    return lax.dot_general(a, b, dims, preferred_element_type=F32)


def call(body, out_shape, operands, after=(), token=False, scratch=(), places=None, outs=None):
    count = len(operands)
    out_shape = tuple(out_shape)
    results = len(out_shape)
    ins = places or [SM] + [VM] * (count - 1)
    outs = outs or (VM,) * results

    moved = sum(v.size * v.dtype.itemsize for v in tuple(operands[1:]) + out_shape)

    def run(*refs):
        given, made = refs[:count], refs[count + len(after) :]
        if token:
            made[results][...] = jnp.zeros((8, 128), F32)
            made = made[:results] + made[results + 1 :]
        body(*given, *made)

    return pl.pallas_call(
        run,
        out_shape=out_shape + ((shape((8, 128), F32),) if token else ()),
        in_specs=list(ins) + [ANY] * len(after),
        out_specs=tuple(outs) + ((VM,) if token else ()),
        scratch_shapes=list(scratch),
        compiler_params=pltpu.CompilerParams(vmem_limit_bytes=VMEM_LIMIT),
        cost_estimate=pl.CostEstimate(flops=0, bytes_accessed=moved, transcendentals=0),
    )(*operands, *after)


def shape(dims, dtype):
    return jax.ShapeDtypeStruct(dims, dtype)


VM = pl.BlockSpec(memory_space=pltpu.VMEM)
SM = pl.BlockSpec(memory_space=pltpu.SMEM)
ANY = pl.BlockSpec(memory_space=pl.ANY)


def owner_of(rows, experts):
    row = lax.broadcasted_iota(jnp.int32, (rows, experts), 0) // CAP
    return (row == lax.broadcasted_iota(jnp.int32, (rows, experts), 1)).astype(F32)


def slot_is(rows, count):
    row = lax.broadcasted_iota(jnp.int32, (rows, count), 0) % CAP
    return row == lax.broadcasted_iota(jnp.int32, (rows, count), 1)


def select_rows(routes, rows, experts):
    topk, count = routes.shape
    expert = lax.broadcasted_iota(jnp.int32, (experts, count), 0)
    named = jnp.zeros((experts, count), F32)
    for k in range(topk):
        named = jnp.where(routes[k : k + 1, :] == expert, 1.0, named)
    earlier = (
        lax.broadcasted_iota(jnp.int32, (count, count), 0) < lax.broadcasted_iota(jnp.int32, (count, count), 1)
    ).astype(F32)
    slot = mm(named.astype(BF), earlier.astype(BF), NN)
    slot = jnp.where(named > 0, slot, 2.0 * CAP)
    owner = owner_of(rows, experts).astype(BF)
    slot_of = mm(owner, slot.astype(BF), NN)
    place = (lax.broadcasted_iota(jnp.int32, (rows, count), 0) % CAP).astype(F32)
    return jnp.where(slot_of == place, 1.0, 0.0)


def weigh_rows(pick, routes, gates):
    topk, count = routes.shape
    rows = pick.shape[0]
    experts = rows // CAP
    expert = lax.broadcasted_iota(jnp.int32, (experts, count), 0)
    weight = jnp.zeros((experts, count), F32)
    for k in range(topk):
        weight = jnp.where(routes[k : k + 1, :] == expert, gates[k : k + 1, :].astype(F32), weight)
    return pick.astype(F32) * mm(owner_of(rows, experts).astype(BF), weight.astype(BF), NN)


def first_body(experts, at, routes, x, out, pick_out):
    pick = select_rows(routes[...], pick_out.shape[0], experts).astype(BF)
    pick_out[...] = pick
    out[...] = mm(pick, x[...], NN).astype(BF)


def rest_body(at, pick, routes, gates, dy, out):
    weighted = weigh_rows(pick[...], routes[...], gates[...]).astype(BF)
    out[...] = mm(weighted, dy[...], NN).astype(BF)


def halves_body(at, gate, up, down, out, token):
    token[...] = jnp.zeros((8, 128), F32)
    units, block = down.shape
    out[0, 0] = gate[...]
    out[0, 1] = up[...]
    for j in range(0, block, units):
        out[0, 2, j : j + units, :] = down[:, j : j + units]


def halves(at, w_gate, w_up, w_down):
    depth, units = w_gate.shape
    block = depth // (2 * CHIPS)
    other = lambda r, at: 2 * ((at[0] + r) % CHIPS) + 1 - at[1]
    tall = pl.BlockSpec((block, units), lambda r, at: (other(r, at), 0))
    wide = pl.BlockSpec((units, block), lambda r, at: (0, other(r, at)))
    return pl.pallas_call(
        halves_body,
        out_shape=(shape((CHIPS, 3, block, units), BF), shape((8, 128), F32)),
        compiler_params=pltpu.CompilerParams(vmem_limit_bytes=VMEM_LIMIT),
        cost_estimate=pl.CostEstimate(flops=0, bytes_accessed=12 * depth * units, transcendentals=0),
        grid_spec=pltpu.PrefetchScalarGridSpec(
            num_scalar_prefetch=1,
            grid=(CHIPS,),
            in_specs=[tall, tall, wide],
            out_specs=[
                pl.BlockSpec((1, 3, block, units), lambda r, at: (r, 0, 0, 0)),
                pl.BlockSpec((8, 128), lambda r, at: (0, 0)),
            ],
        ),
    )(at, w_gate, w_up, w_down)


def block_at(at, r):
    return 2 * lax.rem(at[0] + r, CHIPS) + at[1]


def pre_weights(at, gate, up, others, r, lo, hi):
    block = others.shape[2]
    mine = pl.ds(pl.multiple_of(block_at(at, r) * block + lo, 128), hi - lo)
    return jnp.concatenate([gate[mine, :], others[r, 0, lo:hi, :], up[mine, :], others[r, 1, lo:hi, :]], axis=1)


def down_weights(at, down, others, r, lo, hi):
    units = down.shape[0]
    block = others.shape[2]
    mine = pl.ds(pl.multiple_of(block_at(at, r) * block + lo, 128), hi - lo)
    other = [others[r, 2, j : j + units, :] for j in range(lo, hi, units)]
    return jnp.concatenate([down[:, mine], jnp.concatenate(other, axis=1)], axis=0)


def halves_of(parts, r, half):
    if r == 2:
        return ((0, parts[3][...]), (half, parts[4][...]))
    ref = parts[{0: 0, 1: 1, 3: 2}[r]]
    return ((0, ref[:half, :]), (half, ref[half:, :]))


def swapped(value, units):
    pieces = [value[:, i : i + units] for i in range(0, value.shape[1], units)]
    return jnp.concatenate([pieces[i ^ 1] for i in range(len(pieces))], axis=1).astype(BF)


def add_body(which, first, pre, at, *refs):
    weights, refs = (refs[:3], refs[3:]) if pre else (refs[:2], refs[2:])
    given = 3 * (which[0] == 0) + 2 * (2 in which)
    parts, refs = refs[:given], refs[given:]
    parts = [None] * (5 - given) + list(parts) if which[0] == 2 else parts
    before, refs = (None, refs) if first else (refs[0], refs[1:])
    keep = refs[0]
    half = keep.shape[0] // 2
    for r in which:
        width = weights[-1].shape[2]
        block = pre_weights(at, *weights, r, 0, width) if pre else down_weights(at, *weights, r, 0, width)
        for lo, part in halves_of(parts, r, half):
            value = mm(part, block, NN if pre else NT)
            if r == which[0]:
                keep[lo : lo + half, :] = value if first else before[lo : lo + half, :] + value
            else:
                keep[lo : lo + half, :] += value


def split_body(at, left, right, out_a, out_b):
    half = left.shape[0] // 2
    out_a[...] = left[:half, :]
    out_b[...] = right[half:, :]


def turn_body(at, own, right, left, gate, up, others, out_a, out_b, pre):
    split_body(at, left, right, out_a, out_b)
    add_body((0, 1, 3), True, True, at, gate, up, others, own, right, left, pre)


def early_body(at, gate, up, others, down, *refs):
    far, before, dy, (pre, back, pre_send) = refs[:2], refs[2], refs[3:6], refs[6:]
    add_body((2,), False, True, at, gate, up, others, *far, before, pre)
    pre_send[...] = swapped(pre[...], down.shape[0])
    add_body((0, 1, 3), True, False, at, down, others, *dy, back)


def late_body(at, down, others, opp_a, opp_b, before, back, send):
    add_body((2,), False, False, at, down, others, opp_a, opp_b, before, back)
    send[...] = swapped(back[...], down.shape[0])


def middle_body(at, pre, back, pre_recv, back_recv, gate, up, others, d, act_rows, values, opp_a, opp_b):
    rows = pre.shape[0]
    both = pre.shape[1] // 2
    half = rows // 2
    weights = pre_weights(at, gate, up, others, 2, 0, opp_a.shape[1])
    for lo, out in ((0, opp_a), (half, opp_b)):
        span = slice(lo, lo + half)
        pre_all = pre[span, :] + pre_recv[span, :].astype(F32)
        back_all = back[span, :] + back_recv[span, :].astype(F32)
        pre_gate = pre_all[:, :both]
        pre_up = pre_all[:, both:]
        sig = jax.nn.sigmoid(pre_gate)
        silu = pre_gate * sig
        act = silu * pre_up
        act_rows[span, :] = act.astype(BF)
        d_gate = (back_all * pre_up * (sig * (1.0 + pre_gate * (1.0 - sig)))).astype(BF)
        d_up = (back_all * silu).astype(BF)
        grads = jnp.concatenate([d_gate, d_up], axis=1)
        d[span, :] = grads
        out[...] = mm(grads, weights, NT).astype(BF)
        value = jnp.sum(act * back_all, axis=1, keepdims=True)
        values[span, :] = jnp.broadcast_to(value, (half, values.shape[1]))


def rows_body(at, d, values, gate, up, others, to_right, to_left, right_later, left_later, own, sums):
    half = d.shape[0] // 2
    block = own.shape[1]
    weights = pre_weights(at, gate, up, others, 1, 0, block)
    to_right[...] = mm(d[half:, :], weights, NT).astype(BF)
    right_later[...] = mm(d[:half, :], weights, NT)
    weights = pre_weights(at, gate, up, others, 3, 0, block)
    to_left[...] = mm(d[:half, :], weights, NT).astype(BF)
    left_later[...] = mm(d[half:, :], weights, NT)
    weights = pre_weights(at, gate, up, others, 0, 0, block)
    own[:half, :] = mm(d[:half, :], weights, NT)
    own[half:, :] = mm(d[half:, :], weights, NT)
    rows = d.shape[0]
    sums[...] = lax.dot_general(
        owner_of(rows, rows // CAP),
        jnp.where(slot_is(rows, CAP), values[:, :CAP], 0.0),
        TN,
        preferred_element_type=F32,
        precision=lax.Precision.HIGHEST,
    )


def later_body(at, right_later, left_later, from_left, from_right, to_right, to_left):
    to_right[...] = (right_later[...] + from_left[...].astype(F32)).astype(BF)
    to_left[...] = (left_later[...] + from_right[...].astype(F32)).astype(BF)


def total_body(at, own, left_a, left_b, right_a, right_b, out):
    half = own.shape[0] // 2
    for span, left, right in ((slice(0, half), left_a, right_a), (slice(half, 2 * half), left_b, right_b)):
        out[span, :] = (own[span, :] + left[...].astype(F32) + right[...].astype(F32)).astype(BF)


def grads_body(at, d, act_rows, *refs):
    x, dy, (keep, send) = refs[:5], refs[5:10], refs[10:]
    block, units = keep.shape[2:]
    half = d.shape[0] // 2
    for r in range(CHIPS):
        total = None
        for lo, part in halves_of(x, r, half):
            value = mm(part, d[lo : lo + half, :], TN)
            total = value if total is None else total + value
        for i, (out, kind) in enumerate(((keep, 0), (send, 0), (keep, 1), (send, 1))):
            out[r, kind] = total[:, i * units : (i + 1) * units].astype(BF)
        total = None
        for lo, part in halves_of(dy, r, half):
            value = mm(act_rows[lo : lo + half, :], part, TN)
            total = value if total is None else total + value
        total = total.astype(BF)
        for j in range(0, block, units):
            keep[r, 2, j : j + units, :] = total[:units, j : j + units]
            send[r, 2, j : j + units, :] = total[units:, j : j + units]


def place_body(at, keep, recv, gate, up, down, token):
    token[...] = jnp.zeros((8, 128), F32)
    units = gate.shape[1]
    mine = lax.rem(pl.program_id(0), 2) == at[1]

    def put(held):
        gate[...] = held[0, 0]
        up[...] = held[0, 1]
        for j in range(0, gate.shape[0], units):
            down[:, j : j + units] = held[0, 2, j : j + units, :]

    @pl.when(mine)
    def _():
        put(keep)

    @pl.when(jnp.logical_not(mine))
    def _():
        put(recv)


def place(at, keep, recv):
    _, _, block, units = keep.shape
    depth = 2 * CHIPS * block
    source = pl.BlockSpec((1, 3, block, units), lambda b, at: ((b // 2 + CHIPS - at[0]) % CHIPS, 0, 0, 0))
    return pl.pallas_call(
        place_body,
        out_shape=(
            shape((depth, units), BF),
            shape((depth, units), BF),
            shape((units, depth), BF),
            shape((8, 128), F32),
        ),
        compiler_params=pltpu.CompilerParams(vmem_limit_bytes=VMEM_LIMIT),
        cost_estimate=pl.CostEstimate(flops=0, bytes_accessed=12 * depth * units, transcendentals=0),
        grid_spec=pltpu.PrefetchScalarGridSpec(
            num_scalar_prefetch=1,
            grid=(2 * CHIPS,),
            in_specs=[source, source],
            out_specs=[
                pl.BlockSpec((block, units), lambda b, at: (b, 0)),
                pl.BlockSpec((block, units), lambda b, at: (b, 0)),
                pl.BlockSpec((units, block), lambda b, at: (0, b)),
                pl.BlockSpec((8, 128), lambda b, at: (0, 0)),
            ],
        ),
    )(at, keep, recv)


def finish_body(at, pick, back, grad):
    grad[...] = mm(pick[...], back[...], TN).astype(BF)


def gating_body(at, pick, routes, gates, sums, left, far, right, grad):
    topk, count = routes.shape
    rows = pick.shape[0]
    experts = rows // CAP
    owner = owner_of(rows, experts)
    spread = lax.dot_general(
        owner, sums[...] + left[...] + far[...] + right[...], NN, preferred_element_type=F32, precision=lax.Precision.HIGHEST
    )
    value = jnp.sum(jnp.where(slot_is(rows, CAP), spread, 0.0), axis=1, keepdims=True)
    table = lax.dot_general(
        owner, pick[...].astype(F32) * value, TN, preferred_element_type=F32, precision=lax.Precision.HIGHEST
    )
    expert = lax.broadcasted_iota(jnp.int32, (experts, count), 0)
    for k in range(topk):
        hit = routes[k : k + 1, :] == expert
        picked = jnp.sum(jnp.where(hit, table, 0.0), axis=0, keepdims=True)
        grad[k : k + 1, :] = picked / gates[k : k + 1, :].astype(F32)


def to(value, shift):
    size = 2 * CHIPS
    return lax.ppermute(value, "hidden", [(i, (i + 2 * shift) % size) for i in range(size)])


def swap(value):
    return lax.ppermute(value, "hidden", [(i, i ^ 1) for i in range(2 * CHIPS)])


def behind(value, token):
    return pl.pallas_call(
        lambda *refs: None,
        out_shape=shape(value.shape, value.dtype),
        in_specs=[ANY, ANY],
        out_specs=ANY,
        input_output_aliases={0: 0},
        compiler_params=pltpu.CompilerParams(vmem_limit_bytes=VMEM_LIMIT // 4),
    )(value, token)


def local(tokens, grad_out, routes, gating, w_gate, w_up, w_down):
    experts = lax.axis_size("expert")
    hidden = lax.axis_index("hidden")
    at = jnp.stack([lax.shift_right_logical(hidden, 1), lax.bitwise_and(hidden, 1)]).astype(jnp.int32)
    rows = experts * CAP
    half = rows // 2
    count, width = tokens.shape
    topk = routes.shape[1]
    block = width // (2 * CHIPS)
    gate, up, down = w_gate[0], w_up[0], w_down[0]
    units = gate.shape[1]
    both = 2 * units
    routes, gates = routes.T, gating.T

    def over_experts(value):
        split = value.reshape(experts, value.shape[0] // experts, value.shape[1])
        return lax.all_to_all(split, "expert", split_axis=0, concat_axis=0, tiled=True).reshape(value.shape)

    def my_block(value):
        return lax.dynamic_slice(value, (0, hidden * block), (count, block))

    message, pick = call(
        functools.partial(first_body, experts),
        (shape((rows, block), BF), shape((rows, count), BF)),
        (at, routes, my_block(tokens)),
    )
    arrived = [over_experts(message)]
    halved, token = halves(at, gate, up, down)
    (message,) = call(
        rest_body, (shape((rows, block), BF),), (at, pick, routes, gates, my_block(grad_out)), after=(token,)
    )
    arrived.append(over_experts(message))
    others = swap(halved)
    weights = (gate, up, others)
    part = (shape((half, block), BF),)

    left, right = to(arrived[0], 1), to(arrived[0], -1)
    pass_a, pass_b, pre, *token = call(
        turn_body,
        part * 2 + (shape((rows, 2 * both), F32),),
        (at, arrived[0], right, left, *weights),
        token=True,
    )
    x = (arrived[0], right, left, to(pass_a, 1), to(pass_b, -1))
    left, right = to(arrived[1], 1), to(arrived[1], -1)
    pass_a, pass_b, *token = call(split_body, part * 2, (at, left, right), after=token, token=True)
    dy = (arrived[1], right, left, to(pass_a, 1), to(pass_b, -1))

    narrow = shape((rows, both), F32)
    pre, back, pre_send = call(
        early_body,
        (shape((rows, 2 * both), F32), narrow, shape((rows, 2 * both), BF)),
        (at, *weights, down, *x[3:], pre, *dy[:3]),
        after=token,
    )
    back, send = call(
        late_body,
        (narrow, shape((rows, both), BF)),
        (at, down, others, *dy[3:], back),
    )
    pre_recv, back_recv = swap(pre_send), swap(send)

    later = (shape((half, block), F32),)
    d, act_rows, values, opp_a, opp_b = call(
        middle_body,
        (shape((rows, 2 * both), BF), shape((rows, both), BF), shape((rows, 128), F32)) + part * 2,
        (at, pre, back, pre_recv, back_recv, *weights),
    )
    from_left, from_right = to(opp_a, 1), to(opp_b, -1)
    to_right, to_left, right_later, left_later, own, sums, *token = call(
        rows_body,
        part * 2 + later * 2 + (shape((rows, block), F32), shape((experts, CAP), F32)),
        (at, d, values, *weights),
        token=True,
    )
    left_b, right_a = to(to_right, 1), to(to_left, -1)
    keep, send, *token = call(
        grads_body,
        (shape((CHIPS, 3, block, units), BF),) * 2,
        (at, d, act_rows, *x, *dy),
        after=token,
        token=True,
    )
    to_right, to_left = call(later_body, part * 2, (at, right_later, left_later, from_left, from_right), after=token)
    left_a, right_b = to(to_right, 1), to(to_left, -1)
    slots = over_experts(sums)
    total, *token = call(
        total_body,
        (shape((rows, block), BF),),
        (at, own, left_a, left_b, right_a, right_b),
        after=(slots,),
        token=True,
    )
    returned = over_experts(total)
    *grads, placed = place(at, keep, swap(behind(send, token[0])))
    grad_gating, gated = call(
        gating_body,
        (shape((topk, count), F32),),
        (at, pick, routes, gates, slots, *[to(slots, shift) for shift in (1, 2, 3)]),
        token=True,
    )
    (grad_tokens,) = call(
        finish_body,
        (shape((count, block), BF),),
        (at, pick, returned),
        after=(gated, placed),
    )
    return (grad_tokens, grad_gating.T, grads[0][None], grads[1][None], grads[2][None])


def solution(mesh):
    placed = (
        P("expert", None),
        P("expert", None),
        P("expert", None),
        P("expert", None),
        P("expert", None, "hidden"),
        P("expert", None, "hidden"),
        P("expert", "hidden", None),
    )
    return jax.shard_map(
        local,
        mesh=mesh,
        in_specs=placed,
        out_specs=(
            P("expert", "hidden"),
            P("expert", None),
            P("expert", None, "hidden"),
            P("expert", None, "hidden"),
            P("expert", "hidden", None),
        ),
        check_vma=False,
    )
```

```python
import functools

import jax
import jax.numpy as jnp
from jax import lax
from jax.experimental import pallas as pl
from jax.experimental.pallas import tpu as pltpu
from jax.sharding import PartitionSpec as P

CAP = 16
CHIPS = 4
BF = jnp.bfloat16
F32 = jnp.float32
VMEM_LIMIT = 16 * 1024 * 1024


NN = (((1,), (0,)), ((), ()))
NT = (((1,), (1,)), ((), ()))
TN = (((0,), (0,)), ((), ()))


def mm(a, b, dims):
    return lax.dot_general(a, b, dims, preferred_element_type=F32)


def call(body, out_shape, operands, after=(), token=False, scratch=(), places=None, outs=None):
    count = len(operands)
    out_shape = tuple(out_shape)
    results = len(out_shape)
    ins = places or [SM] + [VM] * (count - 1)
    outs = outs or (VM,) * results

    moved = sum(v.size * v.dtype.itemsize for v in tuple(operands[1:]) + out_shape)

    def run(*refs):
        given, made = refs[:count], refs[count + len(after) :]
        if token:
            made[results][...] = jnp.zeros((8, 128), F32)
            made = made[:results] + made[results + 1 :]
        body(*given, *made)

    return pl.pallas_call(
        run,
        out_shape=out_shape + ((shape((8, 128), F32),) if token else ()),
        in_specs=list(ins) + [ANY] * len(after),
        out_specs=tuple(outs) + ((VM,) if token else ()),
        scratch_shapes=list(scratch),
        compiler_params=pltpu.CompilerParams(vmem_limit_bytes=VMEM_LIMIT),
        cost_estimate=pl.CostEstimate(flops=0, bytes_accessed=moved, transcendentals=0),
    )(*operands, *after)


def shape(dims, dtype):
    return jax.ShapeDtypeStruct(dims, dtype)


VM = pl.BlockSpec(memory_space=pltpu.VMEM)
SM = pl.BlockSpec(memory_space=pltpu.SMEM)
ANY = pl.BlockSpec(memory_space=pl.ANY)


def owner_of(rows, experts):
    row = lax.broadcasted_iota(jnp.int32, (rows, experts), 0) // CAP
    return (row == lax.broadcasted_iota(jnp.int32, (rows, experts), 1)).astype(F32)


def slot_is(rows, count):
    row = lax.broadcasted_iota(jnp.int32, (rows, count), 0) % CAP
    return row == lax.broadcasted_iota(jnp.int32, (rows, count), 1)


def select_rows(routes, rows, experts):
    topk, count = routes.shape
    expert = lax.broadcasted_iota(jnp.int32, (experts, count), 0)
    named = jnp.zeros((experts, count), F32)
    for k in range(topk):
        named = jnp.where(routes[k : k + 1, :] == expert, 1.0, named)
    earlier = (
        lax.broadcasted_iota(jnp.int32, (count, count), 0) < lax.broadcasted_iota(jnp.int32, (count, count), 1)
    ).astype(F32)
    slot = mm(named.astype(BF), earlier.astype(BF), NN)
    slot = jnp.where(named > 0, slot, 2.0 * CAP)
    owner = owner_of(rows, experts).astype(BF)
    slot_of = mm(owner, slot.astype(BF), NN)
    place = (lax.broadcasted_iota(jnp.int32, (rows, count), 0) % CAP).astype(F32)
    return jnp.where(slot_of == place, 1.0, 0.0)


def weigh_rows(pick, routes, gates):
    topk, count = routes.shape
    rows = pick.shape[0]
    experts = rows // CAP
    expert = lax.broadcasted_iota(jnp.int32, (experts, count), 0)
    weight = jnp.zeros((experts, count), F32)
    for k in range(topk):
        weight = jnp.where(routes[k : k + 1, :] == expert, gates[k : k + 1, :].astype(F32), weight)
    return pick.astype(F32) * mm(owner_of(rows, experts).astype(BF), weight.astype(BF), NN)


def first_body(experts, at, routes, x, out, pick_out):
    pick = select_rows(routes[...], pick_out.shape[0], experts).astype(BF)
    pick_out[...] = pick
    out[...] = mm(pick, x[...], NN).astype(BF)


def rest_body(at, pick, routes, gates, dy, out):
    weighted = weigh_rows(pick[...], routes[...], gates[...]).astype(BF)
    out[...] = mm(weighted, dy[...], NN).astype(BF)


def halves_body(at, gate, up, down, out, token):
    token[...] = jnp.zeros((8, 128), F32)
    units, block = down.shape
    out[0, 0] = gate[...]
    out[0, 1] = up[...]
    for j in range(0, block, units):
        out[0, 2, j : j + units, :] = down[:, j : j + units]


def halves(at, w_gate, w_up, w_down):
    depth, units = w_gate.shape
    block = depth // (2 * CHIPS)
    other = lambda r, at: 2 * ((at[0] + r) % CHIPS) + 1 - at[1]
    tall = pl.BlockSpec((block, units), lambda r, at: (other(r, at), 0))
    wide = pl.BlockSpec((units, block), lambda r, at: (0, other(r, at)))
    return pl.pallas_call(
        halves_body,
        out_shape=(shape((CHIPS, 3, block, units), BF), shape((8, 128), F32)),
        compiler_params=pltpu.CompilerParams(vmem_limit_bytes=VMEM_LIMIT),
        cost_estimate=pl.CostEstimate(flops=0, bytes_accessed=12 * depth * units, transcendentals=0),
        grid_spec=pltpu.PrefetchScalarGridSpec(
            num_scalar_prefetch=1,
            grid=(CHIPS,),
            in_specs=[tall, tall, wide],
            out_specs=[
                pl.BlockSpec((1, 3, block, units), lambda r, at: (r, 0, 0, 0)),
                pl.BlockSpec((8, 128), lambda r, at: (0, 0)),
            ],
        ),
    )(at, w_gate, w_up, w_down)


def block_at(at, r):
    return 2 * lax.rem(at[0] + r, CHIPS) + at[1]


def pre_weights(at, gate, up, others, r, lo, hi):
    block = others.shape[2]
    mine = pl.ds(pl.multiple_of(block_at(at, r) * block + lo, 128), hi - lo)
    return jnp.concatenate([gate[mine, :], others[r, 0, lo:hi, :], up[mine, :], others[r, 1, lo:hi, :]], axis=1)


def down_weights(at, down, others, r, lo, hi):
    units = down.shape[0]
    block = others.shape[2]
    mine = pl.ds(pl.multiple_of(block_at(at, r) * block + lo, 128), hi - lo)
    other = [others[r, 2, j : j + units, :] for j in range(lo, hi, units)]
    return jnp.concatenate([down[:, mine], jnp.concatenate(other, axis=1)], axis=0)


def halves_of(parts, r, half):
    if r == 2:
        return ((0, parts[3][...]), (half, parts[4][...]))
    ref = parts[{0: 0, 1: 1, 3: 2}[r]]
    return ((0, ref[:half, :]), (half, ref[half:, :]))


def swapped(value, units):
    pieces = [value[:, i : i + units] for i in range(0, value.shape[1], units)]
    return jnp.concatenate([pieces[i ^ 1] for i in range(len(pieces))], axis=1).astype(BF)


def add_body(which, first, pre, at, *refs):
    weights, refs = (refs[:3], refs[3:]) if pre else (refs[:2], refs[2:])
    given = 3 * (which[0] == 0) + 2 * (2 in which)
    parts, refs = refs[:given], refs[given:]
    parts = [None] * (5 - given) + list(parts) if which[0] == 2 else parts
    before, refs = (None, refs) if first else (refs[0], refs[1:])
    keep = refs[0]
    half = keep.shape[0] // 2
    for r in which:
        width = weights[-1].shape[2]
        block = pre_weights(at, *weights, r, 0, width) if pre else down_weights(at, *weights, r, 0, width)
        for lo, part in halves_of(parts, r, half):
            value = mm(part, block, NN if pre else NT)
            if r == which[0]:
                keep[lo : lo + half, :] = value if first else before[lo : lo + half, :] + value
            else:
                keep[lo : lo + half, :] += value


def split_body(at, left, right, out_a, out_b):
    half = left.shape[0] // 2
    out_a[...] = left[:half, :]
    out_b[...] = right[half:, :]


def turn_body(at, own, right, left, gate, up, others, out_a, out_b, pre):
    split_body(at, left, right, out_a, out_b)
    add_body((0, 1, 3), True, True, at, gate, up, others, own, right, left, pre)


def early_body(at, gate, up, others, down, *refs):
    far, before, dy, (pre, back, pre_send) = refs[:2], refs[2], refs[3:6], refs[6:]
    add_body((2,), False, True, at, gate, up, others, *far, before, pre)
    pre_send[...] = swapped(pre[...], down.shape[0])
    add_body((0, 1, 3), True, False, at, down, others, *dy, back)


def late_body(at, down, others, opp_a, opp_b, before, back, send):
    add_body((2,), False, False, at, down, others, opp_a, opp_b, before, back)
    send[...] = swapped(back[...], down.shape[0])


def middle_body(at, pre, back, pre_recv, back_recv, gate, up, others, d, act_rows, values, opp_a, opp_b):
    rows = pre.shape[0]
    both = pre.shape[1] // 2
    half = rows // 2
    weights = pre_weights(at, gate, up, others, 2, 0, opp_a.shape[1])
    for lo, out in ((0, opp_a), (half, opp_b)):
        span = slice(lo, lo + half)
        pre_all = pre[span, :] + pre_recv[span, :].astype(F32)
        back_all = back[span, :] + back_recv[span, :].astype(F32)
        pre_gate = pre_all[:, :both]
        pre_up = pre_all[:, both:]
        sig = jax.nn.sigmoid(pre_gate)
        silu = pre_gate * sig
        act = silu * pre_up
        act_rows[span, :] = act.astype(BF)
        d_gate = (back_all * pre_up * (sig * (1.0 + pre_gate * (1.0 - sig)))).astype(BF)
        d_up = (back_all * silu).astype(BF)
        grads = jnp.concatenate([d_gate, d_up], axis=1)
        d[span, :] = grads
        out[...] = mm(grads, weights, NT).astype(BF)
        value = jnp.sum(act * back_all, axis=1, keepdims=True)
        values[span, :] = jnp.broadcast_to(value, (half, values.shape[1]))


def rows_body(at, d, values, gate, up, others, to_right, to_left, right_later, left_later, own, sums):
    half = d.shape[0] // 2
    block = own.shape[1]
    weights = pre_weights(at, gate, up, others, 1, 0, block)
    to_right[...] = mm(d[half:, :], weights, NT).astype(BF)
    right_later[...] = mm(d[:half, :], weights, NT)
    weights = pre_weights(at, gate, up, others, 3, 0, block)
    to_left[...] = mm(d[:half, :], weights, NT).astype(BF)
    left_later[...] = mm(d[half:, :], weights, NT)
    weights = pre_weights(at, gate, up, others, 0, 0, block)
    own[:half, :] = mm(d[:half, :], weights, NT)
    own[half:, :] = mm(d[half:, :], weights, NT)
    rows = d.shape[0]
    sums[...] = lax.dot_general(
        owner_of(rows, rows // CAP),
        jnp.where(slot_is(rows, CAP), values[:, :CAP], 0.0),
        TN,
        preferred_element_type=F32,
        precision=lax.Precision.HIGHEST,
    )


def later_body(at, right_later, left_later, from_left, from_right, to_right, to_left):
    to_right[...] = (right_later[...] + from_left[...].astype(F32)).astype(BF)
    to_left[...] = (left_later[...] + from_right[...].astype(F32)).astype(BF)


def total_body(at, own, left_a, left_b, right_a, right_b, out):
    half = own.shape[0] // 2
    for span, left, right in ((slice(0, half), left_a, right_a), (slice(half, 2 * half), left_b, right_b)):
        out[span, :] = (own[span, :] + left[...].astype(F32) + right[...].astype(F32)).astype(BF)


def grads_body(at, d, *refs):
    x, (keep, send) = refs[:5], refs[5:]
    units = keep.shape[3]
    half = d.shape[0] // 2
    for r in range(CHIPS):
        total = None
        for lo, part in halves_of(x, r, half):
            value = mm(part, d[lo : lo + half, :], TN)
            total = value if total is None else total + value
        for i, (out, kind) in enumerate(((keep, 0), (send, 0), (keep, 1), (send, 1))):
            out[r, kind] = total[:, i * units : (i + 1) * units].astype(BF)


def down_body(at, act_rows, *refs):
    dy, (keep, send) = refs[:5], refs[5:]
    units = keep.shape[1]
    half = act_rows.shape[0] // 2
    for r in range(CHIPS):
        total = None
        for lo, part in halves_of(dy, r, half):
            value = mm(act_rows[lo : lo + half, :], part, TN)
            total = value if total is None else total + value
        keep[r] = total[:units, :].astype(BF)
        send[r] = total[units:, :].astype(BF)


def place_body(at, keep, recv, down_keep, down_recv, gate, up, down, token):
    token[...] = jnp.zeros((8, 128), F32)
    mine = lax.rem(pl.program_id(0), 2) == at[1]

    def put(tall, wide):
        gate[...] = tall[0, 0]
        up[...] = tall[0, 1]
        down[...] = wide[0]

    @pl.when(mine)
    def _():
        put(keep, down_keep)

    @pl.when(jnp.logical_not(mine))
    def _():
        put(recv, down_recv)


def place(at, keep, recv, down_keep, down_recv):
    _, _, block, units = keep.shape
    depth = 2 * CHIPS * block
    where = lambda b, at: (b // 2 + CHIPS - at[0]) % CHIPS
    source = pl.BlockSpec((1, 2, block, units), lambda b, at: (where(b, at), 0, 0, 0))
    wide = pl.BlockSpec((1, units, block), lambda b, at: (where(b, at), 0, 0))
    return pl.pallas_call(
        place_body,
        out_shape=(
            shape((depth, units), BF),
            shape((depth, units), BF),
            shape((units, depth), BF),
            shape((8, 128), F32),
        ),
        compiler_params=pltpu.CompilerParams(vmem_limit_bytes=VMEM_LIMIT),
        cost_estimate=pl.CostEstimate(flops=0, bytes_accessed=12 * depth * units, transcendentals=0),
        grid_spec=pltpu.PrefetchScalarGridSpec(
            num_scalar_prefetch=1,
            grid=(2 * CHIPS,),
            in_specs=[source, source, wide, wide],
            out_specs=[
                pl.BlockSpec((block, units), lambda b, at: (b, 0)),
                pl.BlockSpec((block, units), lambda b, at: (b, 0)),
                pl.BlockSpec((units, block), lambda b, at: (0, b)),
                pl.BlockSpec((8, 128), lambda b, at: (0, 0)),
            ],
        ),
    )(at, keep, recv, down_keep, down_recv)


def finish_body(at, pick, back, grad):
    grad[...] = mm(pick[...], back[...], TN).astype(BF)


def gating_body(at, pick, routes, gates, sums, left, far, right, grad):
    topk, count = routes.shape
    rows = pick.shape[0]
    experts = rows // CAP
    owner = owner_of(rows, experts)
    spread = lax.dot_general(
        owner, sums[...] + left[...] + far[...] + right[...], NN, preferred_element_type=F32, precision=lax.Precision.HIGHEST
    )
    value = jnp.sum(jnp.where(slot_is(rows, CAP), spread, 0.0), axis=1, keepdims=True)
    table = lax.dot_general(
        owner, pick[...].astype(F32) * value, TN, preferred_element_type=F32, precision=lax.Precision.HIGHEST
    )
    expert = lax.broadcasted_iota(jnp.int32, (experts, count), 0)
    for k in range(topk):
        hit = routes[k : k + 1, :] == expert
        picked = jnp.sum(jnp.where(hit, table, 0.0), axis=0, keepdims=True)
        grad[k : k + 1, :] = picked / gates[k : k + 1, :].astype(F32)


def to(value, shift):
    size = 2 * CHIPS
    return lax.ppermute(value, "hidden", [(i, (i + 2 * shift) % size) for i in range(size)])


def swap(value):
    return lax.ppermute(value, "hidden", [(i, i ^ 1) for i in range(2 * CHIPS)])


def behind(value, token):
    return pl.pallas_call(
        lambda *refs: None,
        out_shape=shape(value.shape, value.dtype),
        in_specs=[ANY, ANY],
        out_specs=ANY,
        input_output_aliases={0: 0},
        compiler_params=pltpu.CompilerParams(vmem_limit_bytes=VMEM_LIMIT // 4),
    )(value, token)


def local(tokens, grad_out, routes, gating, w_gate, w_up, w_down):
    experts = lax.axis_size("expert")
    hidden = lax.axis_index("hidden")
    at = jnp.stack([lax.shift_right_logical(hidden, 1), lax.bitwise_and(hidden, 1)]).astype(jnp.int32)
    rows = experts * CAP
    half = rows // 2
    count, width = tokens.shape
    topk = routes.shape[1]
    block = width // (2 * CHIPS)
    gate, up, down = w_gate[0], w_up[0], w_down[0]
    units = gate.shape[1]
    both = 2 * units
    routes, gates = routes.T, gating.T

    def over_experts(value):
        split = value.reshape(experts, value.shape[0] // experts, value.shape[1])
        return lax.all_to_all(split, "expert", split_axis=0, concat_axis=0, tiled=True).reshape(value.shape)

    def my_block(value):
        return lax.dynamic_slice(value, (0, hidden * block), (count, block))

    message, pick = call(
        functools.partial(first_body, experts),
        (shape((rows, block), BF), shape((rows, count), BF)),
        (at, routes, my_block(tokens)),
    )
    arrived = [over_experts(message)]
    halved, token = halves(at, gate, up, down)
    (message,) = call(
        rest_body, (shape((rows, block), BF),), (at, pick, routes, gates, my_block(grad_out)), after=(token,)
    )
    arrived.append(over_experts(message))
    others = swap(halved)
    weights = (gate, up, others)
    part = (shape((half, block), BF),)

    left, right = to(arrived[0], 1), to(arrived[0], -1)
    pass_a, pass_b, pre, *token = call(
        turn_body,
        part * 2 + (shape((rows, 2 * both), F32),),
        (at, arrived[0], right, left, *weights),
        token=True,
    )
    x = (arrived[0], right, left, to(pass_a, 1), to(pass_b, -1))
    left, right = to(arrived[1], 1), to(arrived[1], -1)
    pass_a, pass_b, *token = call(split_body, part * 2, (at, left, right), after=token, token=True)
    dy = (arrived[1], right, left, to(pass_a, 1), to(pass_b, -1))

    narrow = shape((rows, both), F32)
    pre, back, pre_send = call(
        early_body,
        (shape((rows, 2 * both), F32), narrow, shape((rows, 2 * both), BF)),
        (at, *weights, down, *x[3:], pre, *dy[:3]),
        after=token,
    )
    back, send = call(
        late_body,
        (narrow, shape((rows, both), BF)),
        (at, down, others, *dy[3:], back),
    )
    pre_recv, back_recv = swap(pre_send), swap(send)

    later = (shape((half, block), F32),)
    d, act_rows, values, opp_a, opp_b = call(
        middle_body,
        (shape((rows, 2 * both), BF), shape((rows, both), BF), shape((rows, 128), F32)) + part * 2,
        (at, pre, back, pre_recv, back_recv, *weights),
    )
    from_left, from_right = to(opp_a, 1), to(opp_b, -1)
    to_right, to_left, right_later, left_later, own, sums, *token = call(
        rows_body,
        part * 2 + later * 2 + (shape((rows, block), F32), shape((experts, CAP), F32)),
        (at, d, values, *weights),
        token=True,
    )
    left_b, right_a = to(to_right, 1), to(to_left, -1)
    keep, send, *token = call(
        grads_body,
        (shape((CHIPS, 2, block, units), BF),) * 2,
        (at, d, *x),
        after=token,
        token=True,
    )
    to_right, to_left = call(later_body, part * 2, (at, right_later, left_later, from_left, from_right), after=token)
    left_a, right_b = to(to_right, 1), to(to_left, -1)
    slots = over_experts(sums)
    total, *token = call(
        total_body,
        (shape((rows, block), BF),),
        (at, own, left_a, left_b, right_a, right_b),
        after=(slots,),
        token=True,
    )
    returned = over_experts(total)
    down_keep, down_send = call(
        down_body, (shape((CHIPS, units, block), BF),) * 2, (at, act_rows, *dy), after=token
    )
    *grads, placed = place(at, keep, swap(behind(send, token[0])), down_keep, swap(down_send))
    grad_gating, gated = call(
        gating_body,
        (shape((topk, count), F32),),
        (at, pick, routes, gates, slots, *[to(slots, shift) for shift in (1, 2, 3)]),
        token=True,
    )
    (grad_tokens,) = call(
        finish_body,
        (shape((count, block), BF),),
        (at, pick, returned),
        after=(gated, placed),
    )
    return (grad_tokens, grad_gating.T, grads[0][None], grads[1][None], grads[2][None])


def solution(mesh):
    placed = (
        P("expert", None),
        P("expert", None),
        P("expert", None),
        P("expert", None),
        P("expert", None, "hidden"),
        P("expert", None, "hidden"),
        P("expert", "hidden", None),
    )
    return jax.shard_map(
        local,
        mesh=mesh,
        in_specs=placed,
        out_specs=(
            P("expert", "hidden"),
            P("expert", None),
            P("expert", None, "hidden"),
            P("expert", None, "hidden"),
            P("expert", "hidden", None),
        ),
        check_vma=False,
    )
```
